256 devices in a mesh: depth: 8 (over x, core), row: 32 (over y, z).
Axes of the slice: x: 4, y: 4, z: 8, core: 2. Of those that a mesh axis runs over, the one named last changes fastest.
Arguments:
- density: float32 [256, 1024, 2048], P('depth', 'row'), may hold values from 0.1 to 30
- emission: float32 [3], replicated, may hold values from 0.5 to 2
- absorption: float32 [1], replicated, may hold values from 0.15 to 0.6
Outputs:
- frame: float32 [4, 1024, 2048], P(None, 'row', 'depth')
The draws below stay inside these ranges and needn't reach their ends.
All inputs are finite; a program needn't handle non-finite values.
Results may differ from the reference program's by a relative error of at most 0.000035.
Values sent between devices are 32-bit elements; how exact they have to be, the bound alone decides.
A program may use at most 64 MiB of HBM per device.

```python
import math
import jax
import jax.numpy as jnp
from jax import lax

W = 2048
NY = 1024
NZ = 256


def steps_of(key, shape, cuts, least, high):
    def one(position, parts):
        draws = jax.random.uniform(jax.random.fold_in(jax.random.fold_in(key, 6), position), (parts,), jnp.float32, least / len(cuts), high / len(cuts))
        return jnp.repeat(jnp.exp(draws), shape[position] // parts).reshape((-1,) + (1,) * (len(shape) - position - 1))

    level = one(*cuts[0])
    for cut in cuts[1:]:
        level = level * one(*cut)
    return level


def setup_inputs(seed: int = 0) -> dict:
    arg_keys = jax.random.split(jax.random.key(seed), 4)
    density = jnp.clip(jnp.exp(math.log(30.0) - 5.7037825 * jax.random.uniform(arg_keys[0], (NZ, NY, W), jnp.float32) ** steps_of(arg_keys[0], (NZ, NY, W), ((0, 8), (1, 32)), -0.2, 0.2)), 0.1, 30.0)
    emission = jnp.clip(jnp.exp(jax.random.uniform(arg_keys[1], (3,), jnp.float32, math.log(0.5), math.log(2.0))), 0.5, 2.0)
    absorption = jnp.clip(jnp.exp(jax.random.uniform(arg_keys[2], (1,), jnp.float32, math.log(0.15), math.log(0.6))), 0.15, 0.6)
    return dict(density=density, emission=emission, absorption=absorption)


def reference(density, emission, absorption):
    depth_count = density.shape[0]

    def step(z, carry):
        lit, depth_tau = carry
        cur = lax.dynamic_index_in_dim(density, z, 0, keepdims=False)
        before = lax.dynamic_index_in_dim(density, jnp.maximum(z - 1, 0), 0, keepdims=False)
        after = lax.dynamic_index_in_dim(density, jnp.minimum(z + 1, depth_count - 1), 0, keepdims=False)
        before = before * (z > 0).astype(jnp.float32)
        after = after * (z < depth_count - 1).astype(jnp.float32)
        grad_z = (after - before) * 0.5
        padded_y = jnp.pad(cur, ((1, 1), (0, 0)))
        grad_y = (padded_y[2:] - padded_y[:-2]) * 0.5
        padded_x = jnp.pad(cur, ((0, 0), (1, 1)))
        grad_x = (padded_x[:, 2:] - padded_x[:, :-2]) * 0.5
        along = jnp.abs(0.64 * grad_z + 0.6 * grad_y + 0.48 * grad_x)
        shade = 0.25 + 0.75 * along / jnp.sqrt(grad_z * grad_z + grad_y * grad_y + grad_x * grad_x + 1.0)
        tau = absorption[0] * cur / NZ
        alpha = 1.0 - jnp.exp(-tau)
        lit = lit + jnp.exp(-depth_tau) * alpha * shade
        return (lit, depth_tau + tau)
    start = (jnp.zeros(density.shape[1:], jnp.float32), jnp.zeros(density.shape[1:], jnp.float32))
    lit, depth_tau = lax.fori_loop(0, depth_count, step, start)
    color = emission[:, None, None] * lit[None]
    opacity = 1.0 - jnp.exp(-depth_tau)
    return jnp.concatenate([color, opacity[None]], axis=0)
```

```python
import functools
import math

import jax
import jax.numpy as jnp
from jax import lax
from jax.experimental import pallas as pl
from jax.experimental.pallas import tpu as pltpu
from jax.sharding import PartitionSpec as P

MESH = pl.DeviceIdType.MESH
LANES = 128
TOP = 8


def chain(i, values):
    out = values[-1]
    for at in range(len(values) - 2, -1, -1):
        out = jnp.where(i == at, values[at], out)
    return out


def render(
    planes, rows, tiles, depth_total, absorption, density, out, vol, stage, recv,
    local_sem, zlo_send, zlo_recv, zhi_send, zhi_recv, ylo_send, ylo_recv, yhi_send, yhi_recv,
    piece_send, piece_recv,
):
    nd, nr = lax.axis_size("depth"), lax.axis_size("row")
    d, r = lax.axis_index("depth"), lax.axis_index("row")
    per_piece = tiles // nd
    body_z, body_y = pl.ds(1, planes), pl.ds(TOP, rows)

    def columns(xt):
        return pl.ds(pl.multiple_of(xt * LANES, LANES), LANES)

    def local_copy(xt):
        return pltpu.make_async_copy(
            density.at[:, :, columns(xt)], vol.at[xt + 1, body_z, body_y, :], local_sem.at[xt]
        )

    def z_copy(xt, up):
        source, target = (planes - 1, 0) if up else (0, planes + 1)
        send, got = (zlo_send, zlo_recv) if up else (zhi_send, zhi_recv)
        return pltpu.make_async_remote_copy(
            src_ref=density.at[source, :, columns(xt)], dst_ref=vol.at[xt + 1, target, body_y, :],
            send_sem=send.at[xt], recv_sem=got.at[xt],
            device_id={"depth": d + 1 if up else d - 1}, device_id_type=MESH,
        )

    def y_copy(xt, up):
        source, target = (rows - 1, TOP - 1) if up else (0, TOP + rows)
        send, got = (ylo_send, ylo_recv) if up else (yhi_send, yhi_recv)
        return pltpu.make_async_remote_copy(
            src_ref=density.at[:, pl.ds(source, 1), columns(xt)],
            dst_ref=vol.at[xt + 1, body_z, pl.ds(target, 1), :],
            send_sem=send.at[xt], recv_sem=got.at[xt],
            device_id={"row": r + 1 if up else r - 1}, device_id_type=MESH,
        )

    def piece_copy(target):
        return pltpu.make_async_remote_copy(
            src_ref=stage.at[target], dst_ref=recv.at[d],
            send_sem=piece_send.at[target], recv_sem=piece_recv.at[d],
            device_id={"depth": target}, device_id_type=MESH,
        )

    def piece_at(step):
        chip, core = d // 2, d % 2
        apart = chain(step, (2, 2, 1, 3, 1, 3, 0, 0))
        flip = chain(step, (0, 1, 0, 0, 1, 1, 1, 0))
        return (chip + apart) % (nd // 2) * 2 + (core + flip) % 2

    def each(count, body):
        def run(i, carry):
            body(i)
            return carry

        lax.fori_loop(0, count, run, 0)

    barrier = pltpu.get_barrier_semaphore()
    each(tiles, lambda xt: local_copy(xt).start())
    for step in range(1, nd):
        pl.semaphore_signal(barrier, inc=1, device_id={"depth": (d + step) % nd}, device_id_type=MESH)

    for step in (1, nr - 1):
        pl.semaphore_signal(barrier, inc=1, device_id={"row": (r + step) % nr}, device_id_type=MESH)

    vol[0, body_z, body_y, :] = jnp.zeros((planes, rows, LANES), jnp.float32)
    vol[tiles + 1, body_z, body_y, :] = jnp.zeros((planes, rows, LANES), jnp.float32)

    def clear_plane(z):
        def one(xt):
            vol[xt + 1, z, body_y, :] = jnp.zeros((rows, LANES), jnp.float32)

        each(tiles, one)

    def clear_row(y):
        def one(xt):
            vol[xt + 1, body_z, pl.ds(y, 1), :] = jnp.zeros((planes, 1, LANES), jnp.float32)

        each(tiles, one)

    pl.when(d == 0)(lambda: clear_plane(0))
    pl.when(d == nd - 1)(lambda: clear_plane(planes + 1))
    pl.when(r == 0)(lambda: clear_row(TOP - 1))
    pl.when(r == nr - 1)(lambda: clear_row(TOP + rows))

    pl.semaphore_wait(barrier, nd + 1)

    def start_halos(i):
        pl.when(d < nd - 1)(lambda: z_copy(i, True).start())
        pl.when(d > 0)(lambda: z_copy(i, False).start())
        xt = piece_at(i // per_piece) * per_piece + i % per_piece
        pl.when(r < nr - 1)(lambda: y_copy(xt, True).start())
        pl.when(r > 0)(lambda: y_copy(xt, False).start())

    each(tiles, start_halos)

    rate = absorption[0] * (-math.log2(math.e) / depth_total)
    lane = lax.broadcasted_iota(jnp.int32, (8, LANES), 1)
    is_first, is_last = lane == 0, lane == LANES - 1

    def cells(xt, starts):
        count = len(starts)

        def load(tile, z, start):
            return vol[tile, z, pl.ds(start, 8), :]

        def step(z, carry):
            before, cur, total, through, shine = ([*part] for part in carry)
            after = [load(xt + 1, z + 2, s) for s in starts]
            for i, s in enumerate(starts):
                c = cur[i]
                left = pltpu.roll(jnp.where(is_last, load(xt, z + 1, s), c), 1, 1)
                right = pltpu.roll(jnp.where(is_first, load(xt + 2, z + 1, s), c), LANES - 1, 1)
                dx = right - left
                dy = load(xt + 1, z + 1, s + 1) - load(xt + 1, z + 1, s - 1)
                dz = after[i] - before[i]
                along = jnp.abs(dz + 0.9375 * dy + 0.75 * dx)
                shade = along * lax.rsqrt(dz * dz + dy * dy + dx * dx + 4.0)
                total[i] = total[i] + c
                beyond = jnp.exp2(total[i] * rate)
                shine[i] = shine[i] + (through[i] - beyond) * shade
                through[i] = beyond
            return tuple(tuple(part) for part in (cur, after, total, through, shine))

        zero, one = jnp.zeros((8, LANES), jnp.float32), jnp.ones((8, LANES), jnp.float32)
        carry = (
            tuple(load(xt + 1, 0, s) for s in starts), tuple(load(xt + 1, 1, s) for s in starts),
            (zero,) * count, (one,) * count, (zero,) * count,
        )
        _, _, _, through, shine = lax.fori_loop(0, planes, step, carry, unroll=True)
        for i, s in enumerate(starts):
            piece, part = xt // per_piece, xt % per_piece
            stage[piece, 0, part, pl.ds(s - TOP, 8), :] = 0.25 * (1.0 - through[i]) + 0.48 * shine[i]
            stage[piece, 1, part, pl.ds(s - TOP, 8), :] = through[i]

    def inner(xt):
        pl.when(xt == 0)(lambda: local_copy(0).wait())
        pl.when(xt < tiles - 1)(lambda: local_copy(xt + 1).wait())
        pl.when(d > 0)(lambda: z_copy(xt, True).wait_recv())
        pl.when(d < nd - 1)(lambda: z_copy(xt, False).wait_recv())
        cells(xt, [TOP + 8 * i for i in range(1, rows // 8 - 1)])

    each(tiles, inner)

    def edges(i):
        piece = piece_at(i // per_piece)
        xt = piece * per_piece + i % per_piece
        pl.when(r > 0)(lambda: y_copy(xt, True).wait_recv())
        pl.when(r < nr - 1)(lambda: y_copy(xt, False).wait_recv())
        cells(xt, [TOP, TOP + rows - 8])
        ready = i % per_piece == per_piece - 1
        pl.when(ready & (piece != d))(lambda: piece_copy(piece).start())

    each(tiles, edges)

    recv[d] = stage[d]

    def drain(xt):
        pl.when(d < nd - 1)(lambda: z_copy(xt, True).wait_send())
        pl.when(d > 0)(lambda: z_copy(xt, False).wait_send())
        pl.when(r < nr - 1)(lambda: y_copy(xt, True).wait_send())
        pl.when(r > 0)(lambda: y_copy(xt, False).wait_send())

    each(tiles, drain)

    def arrived(step):
        other = (d + step + 1) % nd
        piece_copy(other).wait_send()
        pltpu.make_async_remote_copy(
            src_ref=stage.at[other], dst_ref=recv.at[other],
            send_sem=piece_send.at[other], recv_sem=piece_recv.at[other],
            device_id={"depth": other}, device_id_type=MESH,
        ).wait_recv()

    each(nd - 1, arrived)

    for part in range(per_piece):
        for y in range(0, rows, 8):
            at = pl.ds(y, 8)
            lit, through = recv[0, 0, part, at, :], recv[0, 1, part, at, :]
            for s in range(1, nd):
                lit = lit + through * recv[s, 0, part, at, :]
                through = through * recv[s, 1, part, at, :]
            out[0, at, pl.ds(part * LANES, LANES)] = lit
            out[1, at, pl.ds(part * LANES, LANES)] = through


def per_device(density, emission, absorption):
    nd = lax.axis_size("depth")
    planes, rows, width = density.shape
    tiles = width // LANES
    per_piece = tiles // nd
    sems = pltpu.SemaphoreType.DMA
    image = pl.pallas_call(
        functools.partial(render, planes, rows, tiles, planes * nd),
        out_shape=jax.ShapeDtypeStruct((2, rows, width // nd), jnp.float32),
        in_specs=[pl.BlockSpec(memory_space=pltpu.SMEM), pl.BlockSpec(memory_space=pl.ANY)],
        out_specs=pl.BlockSpec(memory_space=pltpu.VMEM),
        scratch_shapes=[
            pltpu.VMEM((tiles + 2, planes + 2, rows + 2 * TOP, LANES), jnp.float32),
            pltpu.VMEM((nd, 2, per_piece, rows, LANES), jnp.float32),
            pltpu.VMEM((nd, 2, per_piece, rows, LANES), jnp.float32),
            *[sems((tiles,))] * 9,
            *[sems((nd,))] * 2,
        ],
        compiler_params=pltpu.CompilerParams(
            collective_id=0, has_side_effects=True, vmem_limit_bytes=32 * 2**20
        ),
    )(absorption, density)
    lit, through = image[0], image[1]
    channel = lax.broadcasted_iota(jnp.int32, (4, 1, 1), 0)
    gain = jnp.concatenate([emission, jnp.zeros((1,), jnp.float32)])[:, None, None]
    return jnp.where(channel == 3, 1.0 - through[None], gain * lit[None])


def solution(mesh):
    placed = (P("depth", "row", None), P(), P())
    return jax.shard_map(
        per_device, mesh=mesh, in_specs=placed, out_specs=P(None, "row", "depth"), check_vma=False
    )
```

```python
import functools
import math

import jax
import jax.numpy as jnp
from jax import lax
from jax.experimental import pallas as pl
from jax.experimental.pallas import tpu as pltpu
from jax.sharding import PartitionSpec as P

MESH = pl.DeviceIdType.MESH
LANES = 128
TOP = 8
APART = (2, 1, 3, 0)


def chain(i, values):
    out = values[-1]
    for at in range(len(values) - 2, -1, -1):
        out = jnp.where(i == at, values[at], out)
    return out


def each(count, body):
    def run(i, carry):
        body(i)
        return carry

    lax.fori_loop(0, count, run, 0)


def render(
    depth_total, absorption, emission, density, out, vol, near, far, mid, stage, merged, sibling, chips_in,
    local_sem, near_send, near_recv, far_send, far_recv, low_send, low_recv, high_send, high_recv,
    sib_send, sib_recv, out_send, out_recv,
):
    planes, groups, tiles = density.shape[:3]
    rows = 8 * groups
    last = planes - 1
    nd, nr = lax.axis_size("depth"), lax.axis_size("row")
    d, r = lax.axis_index("depth"), lax.axis_index("row")
    chips = nd // 2
    chip, core = d // 2, d % 2
    twin = d + 1 - 2 * core
    per_piece = tiles // nd
    inner_groups, edge_groups = range(1, groups - 1), (0, groups - 1)

    def tiles_of(piece):
        return pl.ds(piece * per_piece, per_piece)

    def local_copy(piece, g):
        return pltpu.make_async_copy(
            density.at[:, g, tiles_of(piece)],
            vol.at[:, pl.ds(piece * per_piece + 1, per_piece), pl.ds(TOP + 8 * g, 8), :],
            local_sem.at[piece, g],
        )

    def z_copy(up):
        send, got = (near_send, near_recv) if up else (far_send, far_recv)
        return pltpu.make_async_remote_copy(
            src_ref=density.at[last if up else 0], dst_ref=near if up else far,
            send_sem=send, recv_sem=got,
            device_id={"depth": d + 1 if up else d - 1}, device_id_type=MESH,
        )

    def y_copy(piece, up):
        g, y, target = (groups - 1, 7, TOP - 1) if up else (0, 0, TOP + rows)
        send, got = (low_send, low_recv) if up else (high_send, high_recv)
        return pltpu.make_async_remote_copy(
            src_ref=density.at[:, g, tiles_of(piece), y, :],
            dst_ref=vol.at[:, pl.ds(piece * per_piece + 1, per_piece), target, :],
            send_sem=send.at[piece], recv_sem=got.at[piece],
            device_id={"row": r + 1 if up else r - 1}, device_id_type=MESH,
        )

    def sibling_copy(target_chip, half):
        return pltpu.make_async_remote_copy(
            src_ref=stage.at[target_chip * 2 + 1 - core, half], dst_ref=sibling.at[target_chip, half],
            send_sem=sib_send.at[target_chip, half], recv_sem=sib_recv.at[target_chip, half],
            device_id={"depth": twin}, device_id_type=MESH,
        )

    def chip_copy(other, half, arriving=False):
        return pltpu.make_async_remote_copy(
            src_ref=merged.at[other, half], dst_ref=chips_in.at[other if arriving else chip, half],
            send_sem=out_send.at[other, half], recv_sem=out_recv.at[other if arriving else chip, half],
            device_id={"depth": other * 2 + core}, device_id_type=MESH,
        )

    def chip_at(step):
        return (chip + chain(step, APART)) % chips

    barrier = pltpu.get_barrier_semaphore()
    for peer in (twin, (d + 2) % nd, (d + 4) % nd, (d + 6) % nd, (d + nd - 1 + 2 * core) % nd):
        pl.semaphore_signal(barrier, inc=1, device_id={"depth": peer}, device_id_type=MESH)
    for peer in ((r + 1) % nr, (r + nr - 1) % nr):
        pl.semaphore_signal(barrier, inc=1, device_id={"row": peer}, device_id_type=MESH)

    def start_local(piece):
        for g in range(groups):
            local_copy(piece, g).start()

    each(nd, start_local)

    blank = jnp.zeros((planes, rows, LANES), jnp.float32)
    vol[:, 0, pl.ds(TOP, rows), :] = blank
    vol[:, tiles + 1, pl.ds(TOP, rows), :] = blank

    def clear_plane(ref):
        ref[...] = jnp.zeros(ref.shape, jnp.float32)

    def clear_row(y):
        def one(z):
            vol[z, :, y, :] = jnp.zeros((tiles + 2, LANES), jnp.float32)

        each(planes, one)

    pl.when(d == 0)(lambda: clear_plane(near))
    pl.when(d == nd - 1)(lambda: clear_plane(far))
    pl.when(r == 0)(lambda: clear_row(TOP - 1))
    pl.when(r == nr - 1)(lambda: clear_row(TOP + rows))

    pl.semaphore_wait(barrier, 7)
    pl.when(d < nd - 1)(lambda: z_copy(True).start())
    pl.when(d > 0)(lambda: z_copy(False).start())

    def piece_at(step):
        return chip_at(step % chips) * 2 + jnp.where(step < chips, 1 - core, core)

    def start_rows(step):
        piece = piece_at(step)
        pl.when(r < nr - 1)(lambda: y_copy(piece, True).start())
        pl.when(r > 0)(lambda: y_copy(piece, False).start())

    each(nd, start_rows)

    rate = absorption[0] * (-math.log2(math.e) / depth_total)
    lane = lax.broadcasted_iota(jnp.int32, (8, LANES), 1)
    is_first, is_last = lane == 0, lane == LANES - 1
    zero, one = jnp.zeros((8, LANES), jnp.float32), jnp.ones((8, LANES), jnp.float32)

    def load(tile, z, g, shift=0):
        return vol[z, tile + 1, pl.ds(TOP + 8 * g + shift, 8), :]

    def shading(unit, z, before, c, after):
        tile, g = unit
        left = pltpu.roll(jnp.where(is_last, load(tile - 1, z, g), c), 1, 1)
        right = pltpu.roll(jnp.where(is_first, load(tile + 1, z, g), c), LANES - 1, 1)
        dx = right - left
        dy = load(tile, z, g, 1) - load(tile, z, g, -1)
        dz = after - before
        along = jnp.abs(dz + 0.9375 * dy + 0.75 * dx)
        return along * lax.rsqrt(dz * dz + dy * dy + dx * dx + 4.0)

    def advance(units, z, carry, after):
        before, cur, total, through, shine = ([*part] for part in carry)
        for i, unit in enumerate(units):
            shade = shading(unit, z, before[i], cur[i], after[i])
            total[i] = total[i] + cur[i]
            beyond = jnp.exp2(total[i] * rate)
            shine[i] = shine[i] + (through[i] - beyond) * shade
            through[i] = beyond
        return tuple(tuple(part) for part in (cur, after, total, through, shine))

    def middle(units, carry):
        def step(z, carry):
            return advance(units, z, carry, [load(t, z + 1, g) for t, g in units])

        return lax.fori_loop(1, last, step, carry, unroll=True)

    def lit_of(through, shine):
        return 0.25 * (1.0 - through) + 0.48 * shine

    for g in range(groups):
        local_copy(0, g).wait()

    def inner(piece):
        @pl.when(piece < nd - 1)
        def _():
            for g in range(groups):
                local_copy(piece + 1, g).wait()

        units = [(piece * per_piece + part, g) for part in range(per_piece) for g in inner_groups]
        first = tuple(load(t, 0, g) for t, g in units)
        carry = (
            first, tuple(load(t, 1, g) for t, g in units), first,
            tuple(jnp.exp2(f * rate) for f in first), (zero,) * len(units),
        )
        _, cur, total, through, shine = middle(units, carry)
        for i, (t, g) in enumerate(units):
            at = pl.ds(8 * (g - 1), 8)
            beyond = jnp.exp2((total[i] + cur[i]) * rate)
            mid[t, 0, at, :] = shine[i]
            mid[t, 1, at, :] = beyond
            mid[t, 2, at, :] = through[i] - beyond

    each(nd, inner)

    def ends(piece):
        for part in range(per_piece):
            for g in inner_groups:
                tile = piece * per_piece + part
                unit, at = (tile, g), pl.ds(8 * (g - 1), 8)
                first = load(tile, 0, g)
                shine = mid[tile, 0, at, :]
                shine += (1.0 - jnp.exp2(first * rate)) * shading(unit, 0, near[g, tile], first, load(tile, 1, g))
                shine += mid[tile, 2, at, :] * shading(
                    unit, last, load(tile, last - 1, g), load(tile, last, g), far[g, tile]
                )
                through = mid[tile, 1, at, :]
                stage[piece, 0, 0, part, at, :] = lit_of(through, shine)
                stage[piece, 0, 1, part, at, :] = through

    def outer(piece):
        units = [(piece * per_piece + part, g) for part in range(per_piece) for g in edge_groups]
        carry = (
            tuple(near[g, t] for t, g in units), tuple(load(t, 0, g) for t, g in units),
            (zero,) * len(units), (one,) * len(units), (zero,) * len(units),
        )
        carry = advance(units, 0, carry, [load(t, 1, g) for t, g in units])
        carry = middle(units, carry)
        _, _, _, through, shine = advance(units, last, carry, [far[g, t] for t, g in units])
        for i, (t, g) in enumerate(units):
            part, at = i // 2, pl.ds(8 * (i % 2), 8)
            stage[piece, 1, 0, part, at, :] = lit_of(through[i], shine[i])
            stage[piece, 1, 1, part, at, :] = through[i]

    def wait_rows(piece):
        pl.when(r > 0)(lambda: y_copy(piece, True).wait_recv())
        pl.when(r < nr - 1)(lambda: y_copy(piece, False).wait_recv())

    def merge(target_chip, half):
        sibling_copy(target_chip, half).wait_recv()
        mine, other = stage.at[target_chip * 2 + core, half], sibling.at[target_chip, half]
        lit, through = mine[0], mine[1]
        lit_other, through_other = other[0], other[1]
        front = core == 0
        lit_all = jnp.where(front, lit, lit_other) + jnp.where(front, through, through_other) * jnp.where(
            front, lit_other, lit
        )
        through_all = through * through_other

        @pl.when(target_chip == chip)
        def _():
            chips_in[chip, half, 0] = lit_all
            chips_in[chip, half, 1] = through_all

        @pl.when(target_chip != chip)
        def _():
            merged[target_chip, half, 0] = lit_all
            merged[target_chip, half, 1] = through_all
            chip_copy(target_chip, half).start()

    pl.when(d > 0)(lambda: z_copy(True).wait_recv())
    pl.when(d < nd - 1)(lambda: z_copy(False).wait_recv())

    def for_sibling(step):
        target = chip_at(step)
        piece = target * 2 + 1 - core
        wait_rows(piece)
        ends(piece_at(2 * step))
        ends(piece_at(2 * step + 1))
        outer(piece)
        sibling_copy(target, 1).start()

        @pl.when(step < chips // 2)
        def _():
            sibling_copy(chip_at(2 * step), 0).start()
            sibling_copy(chip_at(2 * step + 1), 0).start()

    each(chips, for_sibling)
    each(chips, lambda step: merge(chip_at(step), 0))

    def for_chips(step):
        target = chip_at(step)
        piece = target * 2 + core
        wait_rows(piece)
        outer(piece)
        merge(target, 1)

    each(chips, for_chips)

    pl.when(d < nd - 1)(lambda: z_copy(True).wait_send())
    pl.when(d > 0)(lambda: z_copy(False).wait_send())

    def drain(piece):
        pl.when(r < nr - 1)(lambda: y_copy(piece, True).wait_send())
        pl.when(r > 0)(lambda: y_copy(piece, False).wait_send())

    each(nd, drain)

    def drain_sibling(target):
        for half in range(2):
            sibling_copy(target, half).wait_send()

    each(chips, drain_sibling)

    def arrived(step):
        other = (chip + 1 + step) % chips
        for half in range(2):
            chip_copy(other, half).wait_send()
            chip_copy(other, half, arriving=True).wait_recv()

    each(chips - 1, arrived)

    for half, which in enumerate((inner_groups, edge_groups)):
        for part in range(per_piece):
            for i, g in enumerate(which):
                at = pl.ds(8 * i, 8)
                lit, through = chips_in[0, half, 0, part, at, :], chips_in[0, half, 1, part, at, :]
                for s in range(1, chips):
                    lit = lit + through * chips_in[s, half, 0, part, at, :]
                    through = through * chips_in[s, half, 1, part, at, :]
                place = pl.ds(8 * g, 8), pl.ds(part * LANES, LANES)
                for c in range(3):
                    out[(c, *place)] = emission[c] * lit
                out[(3, *place)] = 1.0 - through


def per_device(density, emission, absorption):
    nd = lax.axis_size("depth")
    chips = nd // 2
    planes, rows, width = density.shape
    tiles, groups = width // LANES, rows // 8
    per_piece = tiles // nd
    tiled = density.reshape(planes, groups, 8, tiles, LANES).transpose(0, 1, 3, 2, 4)
    sem, real = pltpu.SemaphoreType.DMA, jnp.float32
    half = (2, 2, per_piece, rows // 2, LANES)
    return pl.pallas_call(
        functools.partial(render, planes * nd),
        out_shape=jax.ShapeDtypeStruct((4, rows, width // nd), real),
        in_specs=[pl.BlockSpec(memory_space=pltpu.SMEM)] * 2 + [pl.BlockSpec(memory_space=pl.ANY)],
        out_specs=pl.BlockSpec(memory_space=pltpu.VMEM),
        scratch_shapes=[
            pltpu.VMEM((planes, tiles + 2, rows + 2 * TOP, LANES), real),
            pltpu.VMEM((groups, tiles, 8, LANES), real),
            pltpu.VMEM((groups, tiles, 8, LANES), real),
            pltpu.VMEM((tiles, 3, rows // 2, LANES), real),
            pltpu.VMEM((nd, *half), real),
            pltpu.VMEM((chips, *half), real),
            pltpu.VMEM((chips, *half), real),
            pltpu.VMEM((chips, *half), real),
            sem((nd, groups)),
            *[sem] * 4,
            *[sem((nd,))] * 4,
            *[sem((chips, 2))] * 4,
        ],
        compiler_params=pltpu.CompilerParams(
            collective_id=0, has_side_effects=True, vmem_limit_bytes=57 * 2**20
        ),
    )(absorption, emission, tiled)


def solution(mesh):
    placed = (P("depth", "row", None), P(), P())
    return jax.shard_map(
        per_device, mesh=mesh, in_specs=placed, out_specs=P(None, "row", "depth"), check_vma=False
    )
```

```python
import functools
import math

import jax
import jax.numpy as jnp
from jax import lax
from jax.experimental import pallas as pl
from jax.experimental.pallas import tpu as pltpu
from jax.sharding import PartitionSpec as P

MESH = pl.DeviceIdType.MESH
LANES = 128
LINE = 8
TOP = 8
APART = (2, 1, 3, 2, 1, 3, 0, 0)


def chain(i, values):
    out = values[-1]
    for at in range(len(values) - 2, -1, -1):
        out = jnp.where(i == at, values[at], out)
    return out


def each(count, body):
    def run(i, carry):
        body(i)
        return carry

    lax.fori_loop(0, count, run, 0)


def render(
    depth_total, absorption, emission_in, density, out, emission, vol, near, far, mid, stage, merged, sibling,
    chips_in, emission_sem, local_sem, near_send, near_recv, far_send, far_recv, low_send, low_recv, high_send, high_recv,
    sib_send, sib_recv, out_send, out_recv,
):
    planes, groups, tiles = density.shape[:3]
    rows = 8 * groups
    body_rows = pl.ds(TOP, rows)
    last = planes - 1
    nd, nr = lax.axis_size("depth"), lax.axis_size("row")
    d, r = lax.axis_index("depth"), lax.axis_index("row")
    chips = nd // 2
    chip, core = d // 2, d % 2
    twin = d + 1 - 2 * core
    per_piece = tiles // nd
    inner_groups, edge_groups = range(1, groups - 1), (0, groups - 1)

    def tiles_of(piece):
        return pl.ds(piece * per_piece, per_piece)

    def local_copy(piece, g):
        return pltpu.make_async_copy(
            density.at[:, g, tiles_of(piece)],
            vol.at[:, pl.ds(piece * per_piece + 1, per_piece), pl.ds(TOP + 8 * g, 8), :],
            local_sem.at[piece],
        )

    def wait_local(piece):
        block = vol.at[:, pl.ds(piece * per_piece + 1, per_piece), body_rows, :]
        pltpu.make_async_copy(block, block, local_sem.at[piece]).wait()

    def z_copy(piece, up):
        send, got = (near_send, near_recv) if up else (far_send, far_recv)
        return pltpu.make_async_remote_copy(
            src_ref=density.at[last if up else 0, :, tiles_of(piece)],
            dst_ref=(near if up else far).at[:, tiles_of(piece)],
            send_sem=send, recv_sem=got.at[piece],
            device_id={"depth": d + 1 if up else d - 1}, device_id_type=MESH,
        )

    def y_copy(piece, up):
        g, y, target = (groups - 1, 7, TOP - 1) if up else (0, 0, TOP + rows)
        send, got = (low_send, low_recv) if up else (high_send, high_recv)
        return pltpu.make_async_remote_copy(
            src_ref=density.at[:, g, tiles_of(piece), y, :],
            dst_ref=vol.at[:, pl.ds(piece * per_piece + 1, per_piece), target, :],
            send_sem=send, recv_sem=got.at[piece],
            device_id={"row": r + 1 if up else r - 1}, device_id_type=MESH,
        )

    def sibling_copy(target_chip, half):
        return pltpu.make_async_remote_copy(
            src_ref=stage.at[target_chip * 2 + 1 - core, half], dst_ref=sibling.at[target_chip, half],
            send_sem=sib_send, recv_sem=sib_recv.at[target_chip, half],
            device_id={"depth": twin}, device_id_type=MESH,
        )

    def chip_copy(other, half, arriving=False):
        return pltpu.make_async_remote_copy(
            src_ref=merged.at[other, half], dst_ref=chips_in.at[other if arriving else chip, half],
            send_sem=out_send, recv_sem=out_recv.at[other if arriving else chip, half],
            device_id={"depth": other * 2 + core}, device_id_type=MESH,
        )

    def order(step, device=d):
        mine = ((step >= chips - 1) & (step < nd - 2)) | (step == nd - 1)
        core = device % 2
        return (device // 2 + chain(step, APART)) % chips, jnp.where(mine, core, 1 - core)

    def piece_at(step, device=d):
        owner_chip, owner_core = order(step, device)
        return owner_chip * 2 + owner_core

    barrier = pltpu.get_barrier_semaphore()
    for peer in (twin, (d + 2) % nd, (d + 4) % nd, (d + 6) % nd, (d + nd - 1 + 2 * core) % nd):
        pl.semaphore_signal(barrier, inc=1, device_id={"depth": peer}, device_id_type=MESH)
    below, above = jnp.where(r > 0, 1, 0), jnp.where(r < nr - 1, 1, 0)

    @pl.when(r > 0)
    def _():
        pl.semaphore_signal(barrier, inc=1, device_id={"row": r - 1}, device_id_type=MESH)

    @pl.when(r < nr - 1)
    def _():
        pl.semaphore_signal(barrier, inc=1, device_id={"row": r + 1}, device_id_type=MESH)

    def start_local(piece):
        for g in range(groups):
            local_copy(piece, g).start()

    each(nd, start_local)
    emission_copy = pltpu.make_async_copy(emission_in, emission, emission_sem)
    emission_copy.start()

    blank = jnp.zeros((planes, rows, LANES), jnp.float32)
    vol[:, 0, pl.ds(TOP, rows), :] = blank
    vol[:, tiles + 1, pl.ds(TOP, rows), :] = blank

    def clear_plane(ref):
        ref[...] = jnp.zeros(ref.shape, jnp.float32)

    def clear_row(y):
        def one(z):
            vol[z, :, y, :] = jnp.zeros((tiles + 2, LANES), jnp.float32)

        each(planes, one)

    pl.when(d == 0)(lambda: clear_plane(near))
    pl.when(d == nd - 1)(lambda: clear_plane(far))
    pl.when(r == 0)(lambda: clear_row(TOP - 1))
    pl.when(r == nr - 1)(lambda: clear_row(TOP + rows))

    def start_halos(step):
        piece = piece_at(step)
        pl.when(d < nd - 1)(lambda: z_copy(piece_at(step, d + 1), True).start())
        pl.when(d > 0)(lambda: z_copy(piece_at(step, d - 1), False).start())
        pl.when(r < nr - 1)(lambda: y_copy(piece, True).start())
        pl.when(r > 0)(lambda: y_copy(piece, False).start())

    def open_links():
        pl.semaphore_wait(barrier, 5 + below + above)
        each(nd, start_halos)

    rate = absorption[0] * (-math.log2(math.e) / depth_total)
    lane = lax.broadcasted_iota(jnp.int32, (8, LANES), 1)
    is_first, is_last = lane == 0, lane == LANES - 1
    zero, one = jnp.zeros((8, LANES), jnp.float32), jnp.ones((8, LANES), jnp.float32)

    def load(tile, z, g, shift=0):
        return vol[z, tile + 1, pl.ds(TOP + 8 * g + shift, 8), :]

    def shading(unit, z, before, c, after):
        tile, g = unit
        left = pltpu.roll(jnp.where(is_last, load(tile - 1, z, g), c), 1, 1)
        right = pltpu.roll(jnp.where(is_first, load(tile + 1, z, g), c), LANES - 1, 1)
        dx = right - left
        dy = load(tile, z, g, 1) - load(tile, z, g, -1)
        dz = after - before
        along = jnp.abs(dz + 0.9375 * dy + 0.75 * dx)
        return along * lax.rsqrt(dz * dz + dy * dy + dx * dx + 4.0)

    def advance(units, z, carry, after):
        before, cur, total, through, shine = ([*part] for part in carry)
        for i, unit in enumerate(units):
            shade = shading(unit, z, before[i], cur[i], after[i])
            total[i] = total[i] + cur[i]
            beyond = jnp.exp2(total[i] * rate)
            shine[i] = shine[i] + (through[i] - beyond) * shade
            through[i] = beyond
        return tuple(tuple(part) for part in (cur, after, total, through, shine))

    def middle(units, carry):
        def step(z, carry):
            return advance(units, z, carry, [load(t, z + 1, g) for t, g in units])

        return lax.fori_loop(1, last, step, carry, unroll=True)

    def half_of(g):
        inside = g in inner_groups
        return int(not inside), pl.ds(8 * (inner_groups if inside else edge_groups).index(g), 8)

    def lit_of(through, shine):
        return 0.25 * (1.0 - through) + 0.48 * shine

    wait_local(0)
    opening = jnp.where((r % LINE == 0) & (r > 0), nd - 2, 0)

    def inner(piece):
        pl.when(piece == opening)(open_links)
        pl.when(piece < nd - 1)(lambda: wait_local(piece + 1))
        units = [(piece * per_piece + part, g) for part in range(per_piece) for g in inner_groups]
        first = tuple(load(t, 0, g) for t, g in units)
        carry = (
            first, tuple(load(t, 1, g) for t, g in units), first,
            tuple(jnp.exp2(f * rate) for f in first), (zero,) * len(units),
        )
        _, cur, total, through, shine = middle(units, carry)
        for i, (t, g) in enumerate(units):
            at = pl.ds(8 * (g - 1), 8)
            beyond = jnp.exp2((total[i] + cur[i]) * rate)
            mid[t, 0, at, :] = shine[i]
            mid[t, 1, at, :] = beyond
            mid[t, 2, at, :] = through[i] - beyond

    each(nd, inner)

    def store(piece, part, g, lit, through):
        half, at = half_of(g)
        stage[piece, half, 0, part, at, :] = lit
        stage[piece, half, 1, part, at, :] = through

    def ends(piece):
        for part in range(per_piece):
            for g in inner_groups:
                tile = piece * per_piece + part
                unit, at = (tile, g), pl.ds(8 * (g - 1), 8)
                first = load(tile, 0, g)
                shine = mid[tile, 0, at, :]
                shine += (1.0 - jnp.exp2(first * rate)) * shading(unit, 0, near[g, tile], first, load(tile, 1, g))
                shine += mid[tile, 2, at, :] * shading(
                    unit, last, load(tile, last - 1, g), load(tile, last, g), far[g, tile]
                )
                through = mid[tile, 1, at, :]
                store(piece, part, g, lit_of(through, shine), through)

    def outer(piece):
        units = [(piece * per_piece + part, g) for part in range(per_piece) for g in edge_groups]
        carry = (
            tuple(near[g, t] for t, g in units), tuple(load(t, 0, g) for t, g in units),
            (zero,) * len(units), (one,) * len(units), (zero,) * len(units),
        )
        carry = advance(units, 0, carry, [load(t, 1, g) for t, g in units])
        carry = middle(units, carry)
        _, _, _, through, shine = advance(units, last, carry, [far[g, t] for t, g in units])
        for i, (t, g) in enumerate(units):
            store(piece, i // 2, g, lit_of(through[i], shine[i]), through[i])

    def merge(target_chip, half):
        sibling_copy(target_chip, half).wait_recv()
        mine, other = stage.at[target_chip * 2 + core, half], sibling.at[target_chip, half]
        lit, through = mine[0], mine[1]
        lit_other, through_other = other[0], other[1]
        front = core == 0
        lit_all = jnp.where(front, lit, lit_other) + jnp.where(front, through, through_other) * jnp.where(
            front, lit_other, lit
        )
        return lit_all, through * through_other

    def dispatch(step, half):
        target, owner = order(step)

        @pl.when(owner != core)
        def _():
            sibling_copy(target, half).start()

        @pl.when((owner == core) & (target != chip))
        def _():
            merged[target, half, 0], merged[target, half, 1] = merge(target, half)
            chip_copy(target, half).start()

    def wait_planes(piece):
        pl.when(d > 0)(lambda: z_copy(piece, True).wait_recv())
        pl.when(d < nd - 1)(lambda: z_copy(piece, False).wait_recv())

    def wait_rows(piece):
        pl.when(r > 0)(lambda: y_copy(piece, True).wait_recv())
        pl.when(r < nr - 1)(lambda: y_copy(piece, False).wait_recv())

    wait_planes(piece_at(0))
    ends(piece_at(0))
    dispatch(0, 0)

    def outer_step(step):
        piece, later = piece_at(step), piece_at(jnp.minimum(step + 1, nd - 1))
        pl.when(step < nd - 1)(lambda: wait_planes(later))
        wait_rows(piece)
        ends(later)
        outer(piece)
        dispatch(step, 1)
        pl.when(step < nd - 1)(lambda: dispatch(step + 1, 0))

    each(nd, outer_step)

    def sent(ref, sem):
        pltpu.make_async_remote_copy(
            src_ref=ref, dst_ref=ref, send_sem=sem, recv_sem=out_recv.at[0, 0],
            device_id={"depth": twin}, device_id_type=MESH,
        ).wait_send()

    pl.when(d < nd - 1)(lambda: sent(near, near_send))
    pl.when(d > 0)(lambda: sent(far, far_send))
    halo_row = vol.at[:, pl.ds(1, tiles), TOP, :]
    pl.when(r < nr - 1)(lambda: sent(halo_row, low_send))
    pl.when(r > 0)(lambda: sent(halo_row, high_send))
    sent(sibling, sib_send)
    emission_copy.wait()

    for half, which in enumerate((inner_groups, edge_groups)):
        chips_in[chip, half, 0], chips_in[chip, half, 1] = merge(chip, half)
        each(chips - 1, lambda step: chip_copy((chip + 1 + step) % chips, half, arriving=True).wait_recv())
        for part in range(per_piece):
            for i, g in enumerate(which):
                at = pl.ds(8 * i, 8)
                lit, through = chips_in[0, half, 0, part, at, :], chips_in[0, half, 1, part, at, :]
                for s in range(1, chips):
                    lit = lit + through * chips_in[s, half, 0, part, at, :]
                    through = through * chips_in[s, half, 1, part, at, :]
                place = pl.ds(8 * g, 8), pl.ds(part * LANES, LANES)
                for c in range(3):
                    out[(c, *place)] = emission[c] * lit
                out[(3, *place)] = 1.0 - through
    sent(merged.at[pl.ds(0, chips - 1)], out_send)


def per_device(density, emission, absorption):
    nd = lax.axis_size("depth")
    chips = nd // 2
    planes, rows, width = density.shape
    tiles, groups = width // LANES, rows // 8
    per_piece = tiles // nd
    tiled = density.reshape(planes, groups, 8, tiles, LANES).transpose(0, 1, 3, 2, 4)
    sem, real = pltpu.SemaphoreType.DMA, jnp.float32
    piece = (2, 2, per_piece, rows // 2, LANES)
    return pl.pallas_call(
        functools.partial(render, planes * nd),
        out_shape=jax.ShapeDtypeStruct((4, rows, width // nd), real),
        in_specs=[pl.BlockSpec(memory_space=pltpu.SMEM)] + [pl.BlockSpec(memory_space=pl.ANY)] * 2,
        out_specs=pl.BlockSpec(memory_space=pltpu.VMEM),
        scratch_shapes=[
            pltpu.SMEM((3,), real),
            pltpu.VMEM((planes, tiles + 2, rows + 2 * TOP, LANES), real),
            pltpu.VMEM((groups, tiles, 8, LANES), real),
            pltpu.VMEM((groups, tiles, 8, LANES), real),
            pltpu.VMEM((tiles, 3, rows // 2, LANES), real),
            pltpu.VMEM((nd, *piece), real),
            pltpu.VMEM((chips, *piece), real),
            pltpu.VMEM((chips, *piece), real),
            pltpu.VMEM((chips, *piece), real),
            sem,
            sem((nd,)),
            *[sem, sem((nd,))] * 4,
            *[sem, sem((chips, 2))] * 2,
        ],
        compiler_params=pltpu.CompilerParams(
            collective_id=0, has_side_effects=True, vmem_limit_bytes=52 * 2**20
        ),
    )(absorption, emission, tiled)


def solution(mesh):
    placed = (P("depth", "row", None), P(), P())
    return jax.shard_map(
        per_device, mesh=mesh, in_specs=placed, out_specs=P(None, "row", "depth"), check_vma=False
    )
```

```python
import functools
import math

import jax
import jax.numpy as jnp
from jax import lax
from jax.experimental import pallas as pl
from jax.experimental.pallas import tpu as pltpu
from jax.sharding import PartitionSpec as P

MESH = pl.DeviceIdType.MESH
LANES = 128
HIGH, LOW, INNER = range(3)
LINE = 8
TOP = 8
APART = (2, 1, 3, 2, 1, 3, 0, 0)


def chain(i, values):
    out = values[-1]
    for at in range(len(values) - 2, -1, -1):
        out = jnp.where(i == at, values[at], out)
    return out


def each(count, body):
    def run(i, carry):
        body(i)
        return carry

    lax.fori_loop(0, count, run, 0)


def render(
    depth_total, absorption, emission_in, density, out, emission, vol, planes_in, mid, stage, merged,
    sibling, chips_in, emission_sem, local_sem, up_send, down_send, planes_recv, low_send, low_recv,
    high_send, high_recv, late_sem, sib_send, sib_recv, sib_own_recv, out_send, out_recv,
):
    planes, groups, tiles = density.shape[:3]
    rows = 8 * groups
    body_rows = pl.ds(TOP, rows)
    last = planes - 1
    nd, nr = lax.axis_size("depth"), lax.axis_size("row")
    d, r = lax.axis_index("depth"), lax.axis_index("row")
    chips = nd // 2
    chip, core = d // 2, d % 2
    twin = d + 1 - 2 * core
    per_piece = tiles // nd
    inner_groups = range(1, groups - 1)
    first_of_line = (r % LINE == 0) & (r > 0)
    last_of_line = (r % LINE == LINE - 1) & (r < nr - 1)
    PARTS = pl.ds(groups - 1, 1), pl.ds(0, 1), pl.ds(1, groups - 2)

    def tiles_of(piece):
        return pl.ds(piece * per_piece, per_piece)

    def local_copy(piece, g):
        return pltpu.make_async_copy(
            density.at[:, g, tiles_of(piece)],
            vol.at[:, pl.ds(piece * per_piece + 1, per_piece), pl.ds(TOP + 8 * g, 8), :],
            local_sem.at[piece],
        )

    def wait_local(piece):
        block = vol.at[:, pl.ds(piece * per_piece + 1, per_piece), body_rows, :]
        pltpu.make_async_copy(block, block, local_sem.at[piece]).wait()

    near, far = planes_in.at[0], planes_in.at[1]

    def z_copy(piece, up):
        return pltpu.make_async_remote_copy(
            src_ref=density.at[last if up else 0, :, tiles_of(piece)],
            dst_ref=(near if up else far).at[:, tiles_of(piece)],
            send_sem=up_send if up else down_send, recv_sem=planes_recv.at[piece],
            device_id={"depth": d + 1 if up else d - 1}, device_id_type=MESH,
        )

    def wait_planes(piece):
        def arrived(ref):
            pltpu.make_async_copy(ref, ref, planes_recv.at[piece]).wait()

        pl.when(d == 0)(lambda: arrived(far.at[:, tiles_of(piece)]))
        pl.when(d == nd - 1)(lambda: arrived(near.at[:, tiles_of(piece)]))
        pl.when((d > 0) & (d < nd - 1))(lambda: arrived(planes_in.at[:, :, tiles_of(piece)]))

    def y_copy(piece, up):
        g, y, target = (groups - 1, 7, TOP - 1) if up else (0, 0, TOP + rows)
        send, got = (low_send, low_recv) if up else (high_send, high_recv)
        return pltpu.make_async_remote_copy(
            src_ref=density.at[:, g, tiles_of(piece), y, :],
            dst_ref=vol.at[:, pl.ds(piece * per_piece + 1, per_piece), target, :],
            send_sem=send, recv_sem=got.at[piece],
            device_id={"row": r + 1 if up else r - 1}, device_id_type=MESH,
        )

    def sibling_copy(target_chip, part):
        return pltpu.make_async_remote_copy(
            src_ref=stage.at[target_chip * 2 + 1 - core, PARTS[part]],
            dst_ref=sibling.at[target_chip, PARTS[part]], send_sem=sib_send,
            recv_sem=sib_recv.at[target_chip, part], device_id={"depth": twin}, device_id_type=MESH,
        )

    def sibling_own_copy(part):
        return pltpu.make_async_remote_copy(
            src_ref=stage.at[twin, PARTS[part]], dst_ref=sibling.at[chip, PARTS[part]],
            send_sem=sib_send, recv_sem=sib_own_recv, device_id={"depth": twin}, device_id_type=MESH,
        )

    def chip_copy(other, part):
        return pltpu.make_async_remote_copy(
            src_ref=merged.at[other, PARTS[part]], dst_ref=chips_in.at[chip, PARTS[part]],
            send_sem=out_send, recv_sem=out_recv, device_id={"depth": other * 2 + core}, device_id_type=MESH,
        )

    def arrived(ref, sem):
        pltpu.make_async_copy(ref, ref, sem).wait()

    def order(step, device=d):
        mine = ((step >= chips - 1) & (step < nd - 2)) | (step == nd - 1)
        core = device % 2
        return (device // 2 + chain(step, APART)) % chips, jnp.where(mine, core, 1 - core)

    def piece_at(step, device=d):
        owner_chip, owner_core = order(step, device)
        return owner_chip * 2 + owner_core

    barrier = pltpu.get_barrier_semaphore()
    for peer in (twin, (d + 2) % nd, (d + 4) % nd, (d + 6) % nd, (d + nd - 1 + 2 * core) % nd):
        pl.semaphore_signal(barrier, inc=1, device_id={"depth": peer}, device_id_type=MESH)
    below = jnp.where((r > 0) & jnp.logical_not(first_of_line), 1, 0)
    above = jnp.where(r < nr - 1, 1, 0)

    @pl.when(r > 0)
    def _():
        pl.semaphore_signal(barrier, inc=1, device_id={"row": r - 1}, device_id_type=MESH)

    @pl.when((r < nr - 1) & jnp.logical_not(last_of_line))
    def _():
        pl.semaphore_signal(barrier, inc=1, device_id={"row": r + 1}, device_id_type=MESH)

    def start_local(piece):
        for g in range(groups):
            local_copy(piece, g).start()

    each(nd, start_local)
    emission_copy = pltpu.make_async_copy(emission_in, emission, emission_sem)
    emission_copy.start()

    blank = jnp.zeros((planes, rows, LANES), jnp.float32)
    vol[:, 0, pl.ds(TOP, rows), :] = blank
    vol[:, tiles + 1, pl.ds(TOP, rows), :] = blank

    def clear_plane(ref):
        ref[...] = jnp.zeros(ref.shape, jnp.float32)

    def clear_row(y):
        def one(z):
            vol[z, :, y, :] = jnp.zeros((tiles + 2, LANES), jnp.float32)

        each(planes, one)

    pl.when(d == 0)(lambda: clear_plane(near))
    pl.when(d == nd - 1)(lambda: clear_plane(far))
    pl.when(r == 0)(lambda: clear_row(TOP - 1))
    pl.when(r == nr - 1)(lambda: clear_row(TOP + rows))

    def start_halos(step):
        piece = piece_at(step)
        pl.when(d < nd - 1)(lambda: z_copy(piece_at(step, d + 1), True).start())
        pl.when(d > 0)(lambda: z_copy(piece_at(step, d - 1), False).start())
        pl.when(r < nr - 1)(lambda: y_copy(piece, True).start())
        pl.when((r > 0) & jnp.logical_not(first_of_line))(lambda: y_copy(piece, False).start())

    def start_late(step):
        y_copy(piece_at(step), False).start()

    def open_late():
        pl.semaphore_wait(late_sem, 1)
        each(nd, start_late)

    pl.semaphore_wait(barrier, 5 + below + above)

    @pl.when(last_of_line)
    def _():
        pl.semaphore_signal(late_sem, inc=1, device_id={"row": r + 1}, device_id_type=MESH)

    each(nd, start_halos)

    rate = absorption[0] * (-math.log2(math.e) / depth_total)
    lane = lax.broadcasted_iota(jnp.int32, (8, LANES), 1)
    is_first, is_last = lane == 0, lane == LANES - 1
    zero, one = jnp.zeros((8, LANES), jnp.float32), jnp.ones((8, LANES), jnp.float32)

    def load(tile, z, g, shift=0):
        return vol[z, tile + 1, pl.ds(TOP + 8 * g + shift, 8), :]

    def shading(unit, z, before, c, after):
        tile, g = unit
        left = pltpu.roll(jnp.where(is_last, load(tile - 1, z, g), c), 1, 1)
        right = pltpu.roll(jnp.where(is_first, load(tile + 1, z, g), c), LANES - 1, 1)
        dx = right - left
        dy = load(tile, z, g, 1) - load(tile, z, g, -1)
        dz = after - before
        along = jnp.abs(dz + 0.9375 * dy + 0.75 * dx)
        return along * lax.rsqrt(dz * dz + dy * dy + dx * dx + 4.0)

    def advance(units, z, carry, after):
        before, cur, total, through, shine = ([*part] for part in carry)
        for i, unit in enumerate(units):
            shade = shading(unit, z, before[i], cur[i], after[i])
            total[i] = total[i] + cur[i]
            beyond = jnp.exp2(total[i] * rate)
            shine[i] = shine[i] + (through[i] - beyond) * shade
            through[i] = beyond
        return tuple(tuple(part) for part in (cur, after, total, through, shine))

    def middle(units, carry):
        def step(z, carry):
            return advance(units, z, carry, [load(t, z + 1, g) for t, g in units])

        return lax.fori_loop(1, last, step, carry, unroll=True)

    def lit_of(through, shine):
        return 0.25 * (1.0 - through) + 0.48 * shine

    wait_local(0)

    def inner(piece):
        pl.when(piece < nd - 1)(lambda: wait_local(piece + 1))
        units = [(piece * per_piece + part, g) for part in range(per_piece) for g in inner_groups]
        first = tuple(load(t, 0, g) for t, g in units)
        carry = (
            first, tuple(load(t, 1, g) for t, g in units), first,
            tuple(jnp.exp2(f * rate) for f in first), (zero,) * len(units),
        )
        _, cur, total, through, shine = middle(units, carry)
        for i, (t, g) in enumerate(units):
            at = pl.ds(8 * (g - 1), 8)
            beyond = jnp.exp2((total[i] + cur[i]) * rate)
            mid[t, 0, at, :] = shine[i]
            mid[t, 1, at, :] = beyond
            mid[t, 2, at, :] = through[i] - beyond

    each(nd, inner)

    def store(piece, side, g, lit, through):
        stage[piece, g, 0, side] = lit
        stage[piece, g, 1, side] = through

    def ends(piece):
        for part in range(per_piece):
            for g in inner_groups:
                tile = piece * per_piece + part
                unit, at = (tile, g), pl.ds(8 * (g - 1), 8)
                first = load(tile, 0, g)
                shine = mid[tile, 0, at, :]
                shine += (1.0 - jnp.exp2(first * rate)) * shading(unit, 0, planes_in[0, g, tile], first, load(tile, 1, g))
                shine += mid[tile, 2, at, :] * shading(
                    unit, last, load(tile, last - 1, g), load(tile, last, g), planes_in[1, g, tile]
                )
                through = mid[tile, 1, at, :]
                store(piece, part, g, lit_of(through, shine), through)

    def outer(piece, g):
        units = [(piece * per_piece + part, g) for part in range(per_piece)]
        carry = (
            tuple(planes_in[0, g, t] for t, g in units), tuple(load(t, 0, g) for t, g in units),
            (zero,) * len(units), (one,) * len(units), (zero,) * len(units),
        )
        carry = advance(units, 0, carry, [load(t, 1, g) for t, g in units])
        carry = middle(units, carry)
        _, _, _, through, shine = advance(units, last, carry, [planes_in[1, g, t] for t, g in units])
        for side in range(per_piece):
            store(piece, side, g, lit_of(through[side], shine[side]), through[side])

    def merge(target_chip, part):
        mine, other = stage.at[target_chip * 2 + core, PARTS[part]], sibling.at[target_chip, PARTS[part]]
        lit, through = mine[:, 0], mine[:, 1]
        lit_other, through_other = other[:, 0], other[:, 1]
        front = core == 0
        lit_all = jnp.where(front, lit, lit_other) + jnp.where(front, through, through_other) * jnp.where(
            front, lit_other, lit
        )
        return lit_all, through * through_other

    def dispatch(step, part):
        target, owner = order(step)

        @pl.when((owner != core) & (target != chip))
        def _():
            sibling_copy(target, part).start()

        @pl.when((owner != core) & (target == chip))
        def _():
            sibling_own_copy(part).start()

        @pl.when((owner == core) & (target != chip))
        def _():
            sibling_copy(target, part).wait_recv()
            merged[target, PARTS[part], 0], merged[target, PARTS[part], 1] = merge(target, part)
            chip_copy(target, part).start()

    wait_planes(piece_at(0))
    ends(piece_at(0))
    dispatch(0, INNER)

    def high_step(step):
        piece, later = piece_at(step), piece_at(jnp.minimum(step + 1, nd - 1))
        pl.when(r < nr - 1)(lambda: y_copy(piece, False).wait_recv())
        ends(later)
        outer(piece, groups - 1)
        dispatch(step, HIGH)
        pl.when(step < nd - 1)(lambda: dispatch(step + 1, INNER))

    def low_step(step):
        piece = piece_at(step)
        pl.when(r > 0)(lambda: y_copy(piece, True).wait_recv())
        outer(piece, 0)
        dispatch(step, LOW)

    def outer_step(i):
        pl.when(first_of_line & (i == 3))(open_late)
        apart = first_of_line | last_of_line
        step = jnp.where(apart, i % nd, i // 2)
        low = jnp.where(first_of_line, i // nd, jnp.where(last_of_line, 1 - i // nd, i % 2))
        leads = low == jnp.where(last_of_line, 1, 0)
        pl.when(leads & (step < nd - 1))(lambda: wait_planes(piece_at(step + 1)))
        pl.when(low == 0)(lambda: high_step(step))
        pl.when(low == 1)(lambda: low_step(step))

    each(2 * nd, outer_step)

    def sent(ref, sem):
        pltpu.make_async_remote_copy(
            src_ref=ref, dst_ref=ref, send_sem=sem, recv_sem=out_recv,
            device_id={"depth": twin}, device_id_type=MESH,
        ).wait_send()

    pl.when(d < nd - 1)(lambda: sent(near, up_send))
    pl.when(d > 0)(lambda: sent(far, down_send))
    halo_row = vol.at[:, pl.ds(1, tiles), TOP, :]
    pl.when(r < nr - 1)(lambda: sent(halo_row, low_send))
    pl.when(r > 0)(lambda: sent(halo_row, high_send))
    sent(sibling, sib_send)
    emission_copy.wait()
    arrived(sibling.at[chip], sib_own_recv)
    for part in (HIGH, LOW, INNER):
        chips_in[chip, PARTS[part], 0], chips_in[chip, PARTS[part], 1] = merge(chip, part)
    others = merged.at[pl.ds(0, chips - 1)]
    sent(others, out_send)
    arrived(others, out_recv)

    def wait_planes(piece):
        pl.when(d > 0)(lambda: z_copy(piece, True).wait_recv())
        pl.when(d < nd - 1)(lambda: z_copy(piece, False).wait_recv())

    for g in range(groups):
        for side in range(per_piece):
            lit, through = chips_in[0, g, 0, side], chips_in[0, g, 1, side]
            for s in range(1, chips):
                lit = lit + through * chips_in[s, g, 0, side]
                through = through * chips_in[s, g, 1, side]
            place = pl.ds(8 * g, 8), pl.ds(side * LANES, LANES)
            for c in range(3):
                out[(c, *place)] = emission[c] * lit
            out[(3, *place)] = 1.0 - through


def per_device(density, emission, absorption):
    nd = lax.axis_size("depth")
    chips = nd // 2
    planes, rows, width = density.shape
    tiles, groups = width // LANES, rows // 8
    per_piece = tiles // nd
    tiled = density.reshape(planes, groups, 8, tiles, LANES).transpose(0, 1, 3, 2, 4)
    sem, real = pltpu.SemaphoreType.DMA, jnp.float32
    piece = (groups, 2, per_piece, 8, LANES)
    return pl.pallas_call(
        functools.partial(render, planes * nd),
        out_shape=jax.ShapeDtypeStruct((4, rows, width // nd), real),
        in_specs=[pl.BlockSpec(memory_space=pltpu.SMEM)] + [pl.BlockSpec(memory_space=pl.ANY)] * 2,
        out_specs=pl.BlockSpec(memory_space=pltpu.VMEM),
        scratch_shapes=[
            pltpu.SMEM((3,), real),
            pltpu.VMEM((planes, tiles + 2, rows + 2 * TOP, LANES), real),
            pltpu.VMEM((2, groups, tiles, 8, LANES), real),
            pltpu.VMEM((tiles, 3, rows // 2, LANES), real),
            pltpu.VMEM((nd, *piece), real),
            pltpu.VMEM((chips, *piece), real),
            pltpu.VMEM((chips, *piece), real),
            pltpu.VMEM((chips, *piece), real),
            sem,
            sem((nd,)),
            *[sem] * 2,
            sem((nd,)),
            *[sem, sem((nd,))] * 2,
            pltpu.SemaphoreType.REGULAR,
            sem,
            sem((chips, 3)),
            *[sem] * 3,
        ],
        compiler_params=pltpu.CompilerParams(
            collective_id=0, has_side_effects=True, vmem_limit_bytes=52 * 2**20
        ),
    )(absorption, *(pltpu.with_memory_space_constraint(x, pltpu.HBM) for x in (emission, tiled)))


def solution(mesh):
    placed = (P("depth", "row", None), P(), P())
    return jax.shard_map(
        per_device, mesh=mesh, in_specs=placed, out_specs=P(None, "row", "depth"), check_vma=False
    )
```

```python
import functools
import math

import jax
import jax.numpy as jnp
from jax import lax
from jax.experimental import pallas as pl
from jax.experimental.pallas import tpu as pltpu
from jax.sharding import PartitionSpec as P

MESH = pl.DeviceIdType.MESH
LANES = 128
HIGH, LOW, INNER = range(3)
LINE = 8
TOP = 8
APART = (2, 1, 3, 2, 1, 3, 0, 0)


def chain(i, values):
    out = values[-1]
    for at in range(len(values) - 2, -1, -1):
        out = jnp.where(i == at, values[at], out)
    return out


def each(count, body):
    def run(i, carry):
        body(i)
        return carry

    lax.fori_loop(0, count, run, 0)


def render(
    depth_total, absorption, emission_in, density, out, emission, vol, planes_in, mid, stage, merged,
    sibling, chips_in, emission_sem, local_sem, up_send, down_send, planes_recv, low_send, low_recv,
    high_send, high_recv, late_sem, twin_sem, sib_send, sib_recv, sib_own_recv, out_send, out_recv,
):
    planes, groups, tiles = density.shape[:3]
    rows = 8 * groups
    body_rows = pl.ds(TOP, rows)
    last = planes - 1
    nd, nr = lax.axis_size("depth"), lax.axis_size("row")
    d, r = lax.axis_index("depth"), lax.axis_index("row")
    chips = nd // 2
    chip, core = d // 2, d % 2
    twin = d + 1 - 2 * core
    per_piece = tiles // nd
    inner_groups = range(1, groups - 1)
    first_of_line = (r % LINE == 0) & (r > 0)
    last_of_line = (r % LINE == LINE - 1) & (r < nr - 1)
    before_last = (r % LINE == LINE - 2) & (r < nr - 2)
    greets, hears = last_of_line & (core == 0), last_of_line & (core == 1)
    PARTS = pl.ds(groups - 1, 1), pl.ds(0, 1), pl.ds(1, groups - 2)

    def tiles_of(piece):
        return pl.ds(piece * per_piece, per_piece)

    def local_copy(piece, g):
        return pltpu.make_async_copy(
            density.at[:, g, tiles_of(piece)],
            vol.at[:, pl.ds(piece * per_piece + 1, per_piece), pl.ds(TOP + 8 * g, 8), :],
            local_sem.at[piece],
        )

    def wait_local(piece):
        block = vol.at[:, pl.ds(piece * per_piece + 1, per_piece), body_rows, :]
        pltpu.make_async_copy(block, block, local_sem.at[piece]).wait()

    near, far = planes_in.at[0], planes_in.at[1]

    def z_copy(piece, up):
        return pltpu.make_async_remote_copy(
            src_ref=density.at[last if up else 0, :, tiles_of(piece)],
            dst_ref=(near if up else far).at[:, tiles_of(piece)],
            send_sem=up_send if up else down_send, recv_sem=planes_recv.at[piece],
            device_id={"depth": d + 1 if up else d - 1}, device_id_type=MESH,
        )

    def wait_planes(piece):
        def arrived(ref):
            pltpu.make_async_copy(ref, ref, planes_recv.at[piece]).wait()

        pl.when(d == 0)(lambda: arrived(far.at[:, tiles_of(piece)]))
        pl.when(d == nd - 1)(lambda: arrived(near.at[:, tiles_of(piece)]))
        pl.when((d > 0) & (d < nd - 1))(lambda: arrived(planes_in.at[:, :, tiles_of(piece)]))

    def y_copy(piece, up):
        g, y, target = (groups - 1, 7, TOP - 1) if up else (0, 0, TOP + rows)
        send, got = (low_send, low_recv) if up else (high_send, high_recv)
        return pltpu.make_async_remote_copy(
            src_ref=density.at[:, g, tiles_of(piece), y, :],
            dst_ref=vol.at[:, pl.ds(piece * per_piece + 1, per_piece), target, :],
            send_sem=send, recv_sem=got.at[piece],
            device_id={"row": r + 1 if up else r - 1}, device_id_type=MESH,
        )

    def sibling_copy(target_chip, part):
        return pltpu.make_async_remote_copy(
            src_ref=stage.at[target_chip * 2 + 1 - core, PARTS[part]],
            dst_ref=sibling.at[target_chip, PARTS[part]], send_sem=sib_send,
            recv_sem=sib_recv.at[target_chip, part], device_id={"depth": twin}, device_id_type=MESH,
        )

    def sibling_own_copy(part):
        return pltpu.make_async_remote_copy(
            src_ref=stage.at[twin, PARTS[part]], dst_ref=sibling.at[chip, PARTS[part]],
            send_sem=sib_send, recv_sem=sib_own_recv, device_id={"depth": twin}, device_id_type=MESH,
        )

    def chip_copy(other, part):
        return pltpu.make_async_remote_copy(
            src_ref=merged.at[other, PARTS[part]], dst_ref=chips_in.at[chip, PARTS[part]],
            send_sem=out_send, recv_sem=out_recv, device_id={"depth": other * 2 + core}, device_id_type=MESH,
        )

    def arrived(ref, sem):
        pltpu.make_async_copy(ref, ref, sem).wait()

    def order(step, device=d):
        mine = ((step >= chips - 1) & (step < nd - 2)) | (step == nd - 1)
        core = device % 2
        return (device // 2 + chain(step, APART)) % chips, jnp.where(mine, core, 1 - core)

    def piece_at(step, device=d):
        owner_chip, owner_core = order(step, device)
        return owner_chip * 2 + owner_core

    barrier = pltpu.get_barrier_semaphore()

    def signal(depth, row):
        pl.semaphore_signal(barrier, inc=1, device_id={"depth": depth, "row": row}, device_id_type=MESH)

    signal(twin, r)
    for apart in range(1, chips):
        signal((chip + apart) % chips * 2 + jnp.where(last_of_line, 1, core), r)
    pl.when(jnp.logical_not(last_of_line))(lambda: signal((d + nd - 1 + 2 * core) % nd, r))
    pl.when(r > 0)(lambda: signal(jnp.where(first_of_line, chip * 2, d), r - 1))
    pl.when((r < nr - 1) & jnp.logical_not(last_of_line))(
        lambda: signal(jnp.where(before_last, chip * 2 + 1, d), r + 1)
    )
    below = jnp.where((r > 0) & jnp.logical_not(first_of_line), 1, 0)
    above = jnp.where(r < nr - 1, 1, 0)

    def start_local(piece):
        for g in range(groups):
            local_copy(piece, g).start()

    each(nd, start_local)
    emission_copy = pltpu.make_async_copy(emission_in, emission, emission_sem)
    emission_copy.start()

    blank = jnp.zeros((planes, rows, LANES), jnp.float32)
    vol[:, 0, pl.ds(TOP, rows), :] = blank
    vol[:, tiles + 1, pl.ds(TOP, rows), :] = blank

    def clear_plane(ref):
        ref[...] = jnp.zeros(ref.shape, jnp.float32)

    def clear_row(y):
        def one(z):
            vol[z, :, y, :] = jnp.zeros((tiles + 2, LANES), jnp.float32)

        each(planes, one)

    pl.when(d == 0)(lambda: clear_plane(near))
    pl.when(d == nd - 1)(lambda: clear_plane(far))
    pl.when(r == 0)(lambda: clear_row(TOP - 1))
    pl.when(r == nr - 1)(lambda: clear_row(TOP + rows))

    def start_halos(step):
        piece = piece_at(step)
        pl.when(d < nd - 1)(lambda: z_copy(piece_at(step, d + 1), True).start())
        pl.when(d > 0)(lambda: z_copy(piece_at(step, d - 1), False).start())
        pl.when((r < nr - 1) & jnp.logical_not(last_of_line))(lambda: y_copy(piece, True).start())
        pl.when((r > 0) & jnp.logical_not(first_of_line))(lambda: y_copy(piece, False).start())

    def start_late(step):
        y_copy(piece_at(step), False).start()

    def open_late():
        pl.semaphore_wait(late_sem, 1)
        each(nd, start_late)

    def tell_twin():
        pl.semaphore_signal(twin_sem, inc=1, device_id={"depth": twin}, device_id_type=MESH)

    @pl.when(jnp.logical_not(hears))
    def _():
        pl.semaphore_wait(barrier, jnp.where(greets, 3, 5 + below + above))

    pl.when(greets)(tell_twin)
    pl.when(hears)(lambda: pl.semaphore_wait(twin_sem, 1))

    @pl.when(last_of_line)
    def _():
        pl.semaphore_signal(late_sem, inc=1, device_id={"row": r + 1}, device_id_type=MESH)
        each(nd, lambda step: y_copy(piece_at(step), True).start())

    @pl.when(hears)
    def _():
        pl.semaphore_wait(barrier, 2 * chips + 1)
        tell_twin()

    pl.when(greets)(lambda: pl.semaphore_wait(twin_sem, 1))
    each(nd, start_halos)

    rate = absorption[0] * (-math.log2(math.e) / depth_total)
    lane = lax.broadcasted_iota(jnp.int32, (8, LANES), 1)
    is_first, is_last = lane == 0, lane == LANES - 1
    zero, one = jnp.zeros((8, LANES), jnp.float32), jnp.ones((8, LANES), jnp.float32)

    def load(tile, z, g, shift=0):
        return vol[z, tile + 1, pl.ds(TOP + 8 * g + shift, 8), :]

    def shading(unit, z, before, c, after):
        tile, g = unit
        left = pltpu.roll(jnp.where(is_last, load(tile - 1, z, g), c), 1, 1)
        right = pltpu.roll(jnp.where(is_first, load(tile + 1, z, g), c), LANES - 1, 1)
        dx = right - left
        dy = load(tile, z, g, 1) - load(tile, z, g, -1)
        dz = after - before
        along = jnp.abs(dz + 0.9375 * dy + 0.75 * dx)
        return along * lax.rsqrt(dz * dz + dy * dy + dx * dx + 4.0)

    def advance(units, z, carry, after):
        before, cur, total, through, shine = ([*part] for part in carry)
        for i, unit in enumerate(units):
            shade = shading(unit, z, before[i], cur[i], after[i])
            total[i] = total[i] + cur[i]
            beyond = jnp.exp2(total[i] * rate)
            shine[i] = shine[i] + (through[i] - beyond) * shade
            through[i] = beyond
        return tuple(tuple(part) for part in (cur, after, total, through, shine))

    def middle(units, carry):
        def step(z, carry):
            return advance(units, z, carry, [load(t, z + 1, g) for t, g in units])

        return lax.fori_loop(1, last, step, carry, unroll=True)

    def lit_of(through, shine):
        return 0.25 * (1.0 - through) + 0.48 * shine

    wait_local(0)

    def inner(piece):
        pl.when(piece < nd - 1)(lambda: wait_local(piece + 1))
        units = [(piece * per_piece + part, g) for part in range(per_piece) for g in inner_groups]
        first = tuple(load(t, 0, g) for t, g in units)
        carry = (
            first, tuple(load(t, 1, g) for t, g in units), first,
            tuple(jnp.exp2(f * rate) for f in first), (zero,) * len(units),
        )
        _, cur, total, through, shine = middle(units, carry)
        for i, (t, g) in enumerate(units):
            at = pl.ds(8 * (g - 1), 8)
            beyond = jnp.exp2((total[i] + cur[i]) * rate)
            mid[t, 0, at, :] = shine[i]
            mid[t, 1, at, :] = beyond
            mid[t, 2, at, :] = through[i] - beyond

    each(nd, inner)

    def store(piece, side, g, lit, through):
        stage[piece, g, 0, side] = lit
        stage[piece, g, 1, side] = through

    def ends(piece):
        for part in range(per_piece):
            for g in inner_groups:
                tile = piece * per_piece + part
                unit, at = (tile, g), pl.ds(8 * (g - 1), 8)
                first = load(tile, 0, g)
                shine = mid[tile, 0, at, :]
                shine += (1.0 - jnp.exp2(first * rate)) * shading(unit, 0, planes_in[0, g, tile], first, load(tile, 1, g))
                shine += mid[tile, 2, at, :] * shading(
                    unit, last, load(tile, last - 1, g), load(tile, last, g), planes_in[1, g, tile]
                )
                through = mid[tile, 1, at, :]
                store(piece, part, g, lit_of(through, shine), through)

    def outer(piece, g):
        units = [(piece * per_piece + part, g) for part in range(per_piece)]
        carry = (
            tuple(planes_in[0, g, t] for t, g in units), tuple(load(t, 0, g) for t, g in units),
            (zero,) * len(units), (one,) * len(units), (zero,) * len(units),
        )
        carry = advance(units, 0, carry, [load(t, 1, g) for t, g in units])
        carry = middle(units, carry)
        _, _, _, through, shine = advance(units, last, carry, [planes_in[1, g, t] for t, g in units])
        for side in range(per_piece):
            store(piece, side, g, lit_of(through[side], shine[side]), through[side])

    def merge(target_chip, part):
        mine, other = stage.at[target_chip * 2 + core, PARTS[part]], sibling.at[target_chip, PARTS[part]]
        lit, through = mine[:, 0], mine[:, 1]
        lit_other, through_other = other[:, 0], other[:, 1]
        front = core == 0
        lit_all = jnp.where(front, lit, lit_other) + jnp.where(front, through, through_other) * jnp.where(
            front, lit_other, lit
        )
        return lit_all, through * through_other

    def dispatch(step, part):
        target, owner = order(step)

        @pl.when((owner != core) & (target != chip))
        def _():
            sibling_copy(target, part).start()

        @pl.when((owner != core) & (target == chip))
        def _():
            sibling_own_copy(part).start()

        @pl.when((owner == core) & (target != chip))
        def _():
            sibling_copy(target, part).wait_recv()
            merged[target, PARTS[part], 0], merged[target, PARTS[part], 1] = merge(target, part)
            chip_copy(target, part).start()

    wait_planes(piece_at(0))
    ends(piece_at(0))
    dispatch(0, INNER)

    def high_step(step):
        piece, later = piece_at(step), piece_at(jnp.minimum(step + 1, nd - 1))
        pl.when(r < nr - 1)(lambda: y_copy(piece, False).wait_recv())
        ends(later)
        outer(piece, groups - 1)
        dispatch(step, HIGH)
        pl.when(step < nd - 1)(lambda: dispatch(step + 1, INNER))

    def low_step(step):
        piece = piece_at(step)
        pl.when(r > 0)(lambda: y_copy(piece, True).wait_recv())
        outer(piece, 0)
        dispatch(step, LOW)

    def outer_step(i):
        pl.when(first_of_line & (i == 2))(open_late)
        apart = first_of_line | last_of_line
        step = jnp.where(apart, i % nd, i // 2)
        low = jnp.where(first_of_line, i // nd, jnp.where(last_of_line, 1 - i // nd, i % 2))
        leads = low == jnp.where(last_of_line, 1, 0)
        pl.when(leads & (step < nd - 1))(lambda: wait_planes(piece_at(step + 1)))
        pl.when(low == 0)(lambda: high_step(step))
        pl.when(low == 1)(lambda: low_step(step))

    each(2 * nd, outer_step)

    def sent(ref, sem):
        pltpu.make_async_remote_copy(
            src_ref=ref, dst_ref=ref, send_sem=sem, recv_sem=out_recv,
            device_id={"depth": twin}, device_id_type=MESH,
        ).wait_send()

    pl.when(d < nd - 1)(lambda: sent(near, up_send))
    pl.when(d > 0)(lambda: sent(far, down_send))
    halo_row = vol.at[:, pl.ds(1, tiles), TOP, :]
    pl.when(r < nr - 1)(lambda: sent(halo_row, low_send))
    pl.when(r > 0)(lambda: sent(halo_row, high_send))
    sent(sibling, sib_send)
    emission_copy.wait()
    arrived(sibling.at[chip], sib_own_recv)
    for part in (HIGH, LOW, INNER):
        chips_in[chip, PARTS[part], 0], chips_in[chip, PARTS[part], 1] = merge(chip, part)
    others = merged.at[pl.ds(0, chips - 1)]
    sent(others, out_send)
    arrived(others, out_recv)

    for g in range(groups):
        for side in range(per_piece):
            lit, through = chips_in[0, g, 0, side], chips_in[0, g, 1, side]
            for s in range(1, chips):
                lit = lit + through * chips_in[s, g, 0, side]
                through = through * chips_in[s, g, 1, side]
            place = pl.ds(8 * g, 8), pl.ds(side * LANES, LANES)
            for c in range(3):
                out[(c, *place)] = emission[c] * lit
            out[(3, *place)] = 1.0 - through


def per_device(density, emission, absorption):
    nd = lax.axis_size("depth")
    chips = nd // 2
    planes, rows, width = density.shape
    tiles, groups = width // LANES, rows // 8
    per_piece = tiles // nd
    tiled = density.reshape(planes, groups, 8, tiles, LANES).transpose(0, 1, 3, 2, 4)
    sem, real = pltpu.SemaphoreType.DMA, jnp.float32
    piece = (groups, 2, per_piece, 8, LANES)
    return pl.pallas_call(
        functools.partial(render, planes * nd),
        out_shape=jax.ShapeDtypeStruct((4, rows, width // nd), real),
        in_specs=[pl.BlockSpec(memory_space=pltpu.SMEM)] + [pl.BlockSpec(memory_space=pl.ANY)] * 2,
        out_specs=pl.BlockSpec(memory_space=pltpu.VMEM),
        scratch_shapes=[
            pltpu.SMEM((3,), real),
            pltpu.VMEM((planes, tiles + 2, rows + 2 * TOP, LANES), real),
            pltpu.VMEM((2, groups, tiles, 8, LANES), real),
            pltpu.VMEM((tiles, 3, rows // 2, LANES), real),
            pltpu.VMEM((nd, *piece), real),
            pltpu.VMEM((chips, *piece), real),
            pltpu.VMEM((chips, *piece), real),
            pltpu.VMEM((chips, *piece), real),
            sem,
            sem((nd,)),
            *[sem] * 2,
            sem((nd,)),
            *[sem, sem((nd,))] * 2,
            *[pltpu.SemaphoreType.REGULAR] * 2,
            sem,
            sem((chips, 3)),
            *[sem] * 3,
        ],
        compiler_params=pltpu.CompilerParams(
            collective_id=0, has_side_effects=True, vmem_limit_bytes=52 * 2**20
        ),
    )(absorption, *(pltpu.with_memory_space_constraint(x, pltpu.HBM) for x in (emission, tiled)))


def solution(mesh):
    placed = (P("depth", "row", None), P(), P())
    return jax.shard_map(
        per_device, mesh=mesh, in_specs=placed, out_specs=P(None, "row", "depth"), check_vma=False
    )
```

```python
import functools
import math

import jax
import jax.numpy as jnp
from jax import lax
from jax.experimental import pallas as pl
from jax.experimental.pallas import tpu as pltpu
from jax.sharding import PartitionSpec as P

MESH = pl.DeviceIdType.MESH
LANES = 128
HIGH, LOW, INNER = range(3)
LINE = 8
TOP = 8
APART = (2, 1, 3, 2, 1, 3, 0, 0)


def chain(i, values):
    out = values[-1]
    for at in range(len(values) - 2, -1, -1):
        out = jnp.where(i == at, values[at], out)
    return out


def lagging(count, lag):
    ahead = [(2 * k, 0, k) for k in range(count)]
    behind = [(2 * (k + lag) - 1, 1, k) for k in range(count)]
    return [turn for _, *turn in sorted(ahead + behind)]


def each(count, body):
    def run(i, carry):
        body(i)
        return carry

    lax.fori_loop(0, count, run, 0)


def render(
    depth_total, absorption, emission_in, density, out, emission, vol, planes_in, mid, stage, merged,
    sibling, chips_in, emission_sem, local_sem, up_send, down_send, planes_recv, low_send, low_recv,
    high_send, high_recv, late_sem, twin_sem, sib_send, sib_recv, sib_own_recv, out_send, out_recv,
):
    planes, groups, tiles = density.shape[:3]
    rows = 8 * groups
    body_rows = pl.ds(TOP, rows)
    last = planes - 1
    nd, nr = lax.axis_size("depth"), lax.axis_size("row")
    d, r = lax.axis_index("depth"), lax.axis_index("row")
    chips = nd // 2
    chip, core = d // 2, d % 2
    twin = d + 1 - 2 * core
    per_piece = tiles // nd
    inner_groups = range(1, groups - 1)
    first_of_line = (r % LINE == 0) & (r > 0)
    last_of_line = (r % LINE == LINE - 1) & (r < nr - 1)
    before_last = (r % LINE == LINE - 2) & (r < nr - 2)
    greets, hears = last_of_line & (core == 0), last_of_line & (core == 1)
    PARTS = pl.ds(groups - 1, 1), pl.ds(0, 1), pl.ds(1, groups - 2)

    def tiles_of(piece):
        return pl.ds(piece * per_piece, per_piece)

    def local_copy(piece, g):
        return pltpu.make_async_copy(
            density.at[:, g, tiles_of(piece)],
            vol.at[:, pl.ds(piece * per_piece + 1, per_piece), pl.ds(TOP + 8 * g, 8), :],
            local_sem.at[piece],
        )

    def wait_local(piece):
        block = vol.at[:, pl.ds(piece * per_piece + 1, per_piece), body_rows, :]
        pltpu.make_async_copy(block, block, local_sem.at[piece]).wait()

    near, far = planes_in.at[0], planes_in.at[1]

    def z_copy(piece, up):
        return pltpu.make_async_remote_copy(
            src_ref=density.at[last if up else 0, :, tiles_of(piece)],
            dst_ref=(near if up else far).at[:, tiles_of(piece)],
            send_sem=up_send if up else down_send, recv_sem=planes_recv.at[piece],
            device_id={"depth": d + 1 if up else d - 1}, device_id_type=MESH,
        )

    def wait_planes(piece):
        def arrived(ref):
            pltpu.make_async_copy(ref, ref, planes_recv.at[piece]).wait()

        pl.when(d == 0)(lambda: arrived(far.at[:, tiles_of(piece)]))
        pl.when(d == nd - 1)(lambda: arrived(near.at[:, tiles_of(piece)]))
        pl.when((d > 0) & (d < nd - 1))(lambda: arrived(planes_in.at[:, :, tiles_of(piece)]))

    def y_copy(piece, up):
        g, y, target = (groups - 1, 7, TOP - 1) if up else (0, 0, TOP + rows)
        send, got = (low_send, low_recv) if up else (high_send, high_recv)
        return pltpu.make_async_remote_copy(
            src_ref=density.at[:, g, tiles_of(piece), y, :],
            dst_ref=vol.at[:, pl.ds(piece * per_piece + 1, per_piece), target, :],
            send_sem=send, recv_sem=got.at[piece],
            device_id={"row": r + 1 if up else r - 1}, device_id_type=MESH,
        )

    def sibling_copy(target_chip, part):
        return pltpu.make_async_remote_copy(
            src_ref=stage.at[target_chip * 2 + 1 - core, PARTS[part]],
            dst_ref=sibling.at[target_chip, PARTS[part]], send_sem=sib_send,
            recv_sem=sib_recv.at[target_chip, part], device_id={"depth": twin}, device_id_type=MESH,
        )

    def sibling_own_copy(part):
        return pltpu.make_async_remote_copy(
            src_ref=stage.at[twin, PARTS[part]], dst_ref=sibling.at[chip, PARTS[part]],
            send_sem=sib_send, recv_sem=sib_own_recv, device_id={"depth": twin}, device_id_type=MESH,
        )

    def chip_copy(other, part):
        return pltpu.make_async_remote_copy(
            src_ref=merged.at[other, PARTS[part]], dst_ref=chips_in.at[chip, PARTS[part]],
            send_sem=out_send, recv_sem=out_recv, device_id={"depth": other * 2 + core}, device_id_type=MESH,
        )

    def arrived(ref, sem):
        pltpu.make_async_copy(ref, ref, sem).wait()

    def order(step, device=d):
        mine = ((step >= chips - 1) & (step < nd - 2)) | (step == nd - 1)
        core = device % 2
        return (device // 2 + chain(step, APART)) % chips, jnp.where(mine, core, 1 - core)

    def piece_at(step, device=d):
        owner_chip, owner_core = order(step, device)
        return owner_chip * 2 + owner_core

    barrier = pltpu.get_barrier_semaphore()

    def signal(depth, row):
        pl.semaphore_signal(barrier, inc=1, device_id={"depth": depth, "row": row}, device_id_type=MESH)

    signal(twin, r)
    for apart in range(1, chips):
        signal((chip + apart) % chips * 2 + jnp.where(last_of_line, 1, core), r)
    pl.when(jnp.logical_not(last_of_line))(lambda: signal((d + nd - 1 + 2 * core) % nd, r))
    pl.when(r > 0)(lambda: signal(jnp.where(first_of_line, chip * 2, d), r - 1))
    pl.when((r < nr - 1) & jnp.logical_not(last_of_line))(
        lambda: signal(jnp.where(before_last, chip * 2 + 1, d), r + 1)
    )
    below = jnp.where((r > 0) & jnp.logical_not(first_of_line), 1, 0)
    above = jnp.where(r < nr - 1, 1, 0)

    def start_local(piece):
        for g in range(groups):
            local_copy(piece, g).start()

    each(nd, start_local)
    emission_copy = pltpu.make_async_copy(emission_in, emission, emission_sem)
    emission_copy.start()

    blank = jnp.zeros((planes, rows, LANES), jnp.float32)
    vol[:, 0, pl.ds(TOP, rows), :] = blank
    vol[:, tiles + 1, pl.ds(TOP, rows), :] = blank

    def clear_plane(ref):
        ref[...] = jnp.zeros(ref.shape, jnp.float32)

    def clear_row(y):
        def one(z):
            vol[z, :, y, :] = jnp.zeros((tiles + 2, LANES), jnp.float32)

        each(planes, one)

    pl.when(d == 0)(lambda: clear_plane(near))
    pl.when(d == nd - 1)(lambda: clear_plane(far))
    pl.when(r == 0)(lambda: clear_row(TOP - 1))
    pl.when(r == nr - 1)(lambda: clear_row(TOP + rows))

    def start_halos(step):
        piece = piece_at(step)
        pl.when(d < nd - 1)(lambda: z_copy(piece_at(step, d + 1), True).start())
        pl.when(d > 0)(lambda: z_copy(piece_at(step, d - 1), False).start())
        pl.when((r < nr - 1) & jnp.logical_not(last_of_line))(lambda: y_copy(piece, True).start())
        pl.when((r > 0) & jnp.logical_not(first_of_line))(lambda: y_copy(piece, False).start())

    def start_late(step):
        y_copy(piece_at(step), False).start()

    def open_late():
        pl.semaphore_wait(late_sem, 1)
        each(nd, start_late)

    def tell_twin():
        pl.semaphore_signal(twin_sem, inc=1, device_id={"depth": twin}, device_id_type=MESH)

    @pl.when(jnp.logical_not(hears))
    def _():
        pl.semaphore_wait(barrier, jnp.where(greets, 3, 5 + below + above))

    pl.when(greets)(tell_twin)
    pl.when(hears)(lambda: pl.semaphore_wait(twin_sem, 1))

    @pl.when(last_of_line)
    def _():
        pl.semaphore_signal(late_sem, inc=1, device_id={"row": r + 1}, device_id_type=MESH)
        each(nd, lambda step: y_copy(piece_at(step), True).start())

    @pl.when(hears)
    def _():
        pl.semaphore_wait(barrier, 2 * chips + 1)
        tell_twin()

    pl.when(greets)(lambda: pl.semaphore_wait(twin_sem, 1))
    each(nd, start_halos)

    rate = absorption[0] * (-math.log2(math.e) / depth_total)
    lane = lax.broadcasted_iota(jnp.int32, (8, LANES), 1)
    is_first, is_last = lane == 0, lane == LANES - 1
    zero, one = jnp.zeros((8, LANES), jnp.float32), jnp.ones((8, LANES), jnp.float32)

    def load(tile, z, g, shift=0):
        return vol[z, tile + 1, pl.ds(TOP + 8 * g + shift, 8), :]

    def shading(unit, z, before, c, after):
        tile, g = unit
        left = pltpu.roll(jnp.where(is_last, load(tile - 1, z, g), c), 1, 1)
        right = pltpu.roll(jnp.where(is_first, load(tile + 1, z, g), c), LANES - 1, 1)
        dx = right - left
        dy = load(tile, z, g, 1) - load(tile, z, g, -1)
        dz = after - before
        along = jnp.abs(dz + 0.9375 * dy + 0.75 * dx)
        return along * lax.rsqrt(dz * dz + dy * dy + dx * dx + 4.0)

    def advance(units, z, carry, after):
        before, cur, total, through, shine = ([*part] for part in carry)
        for i, unit in enumerate(units):
            shade = shading(unit, z, before[i], cur[i], after[i])
            total[i] = total[i] + cur[i]
            beyond = jnp.exp2(total[i] * rate)
            shine[i] = shine[i] + (through[i] - beyond) * shade
            through[i] = beyond
        return tuple(tuple(part) for part in (cur, after, total, through, shine))

    def middle(units, carry):
        def step(z, carry):
            return advance(units, z, carry, [load(t, z + 1, g) for t, g in units])

        return lax.fori_loop(1, last, step, carry, unroll=True)

    def lit_of(through, shine):
        return 0.25 * (1.0 - through) + 0.48 * shine

    wait_local(0)

    def inner(piece):
        pl.when(piece < nd - 1)(lambda: wait_local(piece + 1))
        units = [(piece * per_piece + part, g) for part in range(per_piece) for g in inner_groups]
        first = tuple(load(t, 0, g) for t, g in units)
        carry = (
            first, tuple(load(t, 1, g) for t, g in units), first,
            tuple(jnp.exp2(f * rate) for f in first), (zero,) * len(units),
        )
        _, cur, total, through, shine = middle(units, carry)
        for i, (t, g) in enumerate(units):
            at = pl.ds(8 * (g - 1), 8)
            beyond = jnp.exp2((total[i] + cur[i]) * rate)
            mid[t, 0, at, :] = shine[i]
            mid[t, 1, at, :] = beyond
            mid[t, 2, at, :] = through[i] - beyond

    each(nd, inner)

    def store(piece, side, g, lit, through):
        stage[piece, g, 0, side] = lit
        stage[piece, g, 1, side] = through

    def ends(piece):
        for part in range(per_piece):
            for g in inner_groups:
                tile = piece * per_piece + part
                unit, at = (tile, g), pl.ds(8 * (g - 1), 8)
                first = load(tile, 0, g)
                shine = mid[tile, 0, at, :]
                shine += (1.0 - jnp.exp2(first * rate)) * shading(unit, 0, planes_in[0, g, tile], first, load(tile, 1, g))
                shine += mid[tile, 2, at, :] * shading(
                    unit, last, load(tile, last - 1, g), load(tile, last, g), planes_in[1, g, tile]
                )
                through = mid[tile, 1, at, :]
                store(piece, part, g, lit_of(through, shine), through)

    def outer(piece, g):
        units = [(piece * per_piece + part, g) for part in range(per_piece)]
        carry = (
            tuple(planes_in[0, g, t] for t, g in units), tuple(load(t, 0, g) for t, g in units),
            (zero,) * len(units), (one,) * len(units), (zero,) * len(units),
        )
        carry = advance(units, 0, carry, [load(t, 1, g) for t, g in units])
        carry = middle(units, carry)
        _, _, _, through, shine = advance(units, last, carry, [planes_in[1, g, t] for t, g in units])
        for side in range(per_piece):
            store(piece, side, g, lit_of(through[side], shine[side]), through[side])

    def merge(target_chip, part):
        mine, other = stage.at[target_chip * 2 + core, PARTS[part]], sibling.at[target_chip, PARTS[part]]
        lit, through = mine[:, 0], mine[:, 1]
        lit_other, through_other = other[:, 0], other[:, 1]
        front = core == 0
        lit_all = jnp.where(front, lit, lit_other) + jnp.where(front, through, through_other) * jnp.where(
            front, lit_other, lit
        )
        return lit_all, through * through_other

    def dispatch(step, part):
        target, owner = order(step)

        @pl.when((owner != core) & (target != chip))
        def _():
            sibling_copy(target, part).start()

        @pl.when((owner != core) & (target == chip))
        def _():
            sibling_own_copy(part).start()

        @pl.when((owner == core) & (target != chip))
        def _():
            sibling_copy(target, part).wait_recv()
            merged[target, PARTS[part], 0], merged[target, PARTS[part], 1] = merge(target, part)
            chip_copy(target, part).start()

    wait_planes(piece_at(0))
    ends(piece_at(0))
    dispatch(0, INNER)

    def high_step(step):
        piece, later = piece_at(step), piece_at(jnp.minimum(step + 1, nd - 1))
        pl.when(r < nr - 1)(lambda: y_copy(piece, False).wait_recv())
        ends(later)
        outer(piece, groups - 1)
        dispatch(step, HIGH)
        pl.when(step < nd - 1)(lambda: dispatch(step + 1, INNER))

    def low_step(step):
        piece = piece_at(step)
        pl.when(r > 0)(lambda: y_copy(piece, True).wait_recv())
        outer(piece, 0)
        dispatch(step, LOW)

    def outer_step(i):
        pl.when(first_of_line & (i == 2))(open_late)
        trails, step = i % 2, i // 2
        for rows_of, lag in ((first_of_line, 4), (last_of_line, 3)):
            turns = lagging(nd - 2, lag) + [[side, k] for k in (nd - 2, nd - 1) for side in (0, 1)]
            trails = jnp.where(rows_of, chain(i, [t for t, _ in turns]), trails)
            step = jnp.where(rows_of, chain(i, [k for _, k in turns]), step)
        low = jnp.where(last_of_line, 1 - trails, trails)
        pl.when((trails == 0) & (step < nd - 1))(lambda: wait_planes(piece_at(step + 1)))
        pl.when(low == 0)(lambda: high_step(step))
        pl.when(low == 1)(lambda: low_step(step))

    each(2 * nd, outer_step)

    def sent(ref, sem):
        pltpu.make_async_remote_copy(
            src_ref=ref, dst_ref=ref, send_sem=sem, recv_sem=out_recv,
            device_id={"depth": twin}, device_id_type=MESH,
        ).wait_send()

    pl.when(d < nd - 1)(lambda: sent(near, up_send))
    pl.when(d > 0)(lambda: sent(far, down_send))
    halo_row = vol.at[:, pl.ds(1, tiles), TOP, :]
    pl.when(r < nr - 1)(lambda: sent(halo_row, low_send))
    pl.when(r > 0)(lambda: sent(halo_row, high_send))
    sent(sibling, sib_send)
    emission_copy.wait()
    arrived(sibling.at[chip], sib_own_recv)
    for part in (HIGH, LOW, INNER):
        chips_in[chip, PARTS[part], 0], chips_in[chip, PARTS[part], 1] = merge(chip, part)
    others = merged.at[pl.ds(0, chips - 1)]
    sent(others, out_send)
    arrived(others, out_recv)

    for g in range(groups):
        for side in range(per_piece):
            lit, through = chips_in[0, g, 0, side], chips_in[0, g, 1, side]
            for s in range(1, chips):
                lit = lit + through * chips_in[s, g, 0, side]
                through = through * chips_in[s, g, 1, side]
            place = pl.ds(8 * g, 8), pl.ds(side * LANES, LANES)
            for c in range(3):
                out[(c, *place)] = emission[c] * lit
            out[(3, *place)] = 1.0 - through


def per_device(density, emission, absorption):
    nd = lax.axis_size("depth")
    chips = nd // 2
    planes, rows, width = density.shape
    tiles, groups = width // LANES, rows // 8
    per_piece = tiles // nd
    tiled = density.reshape(planes, groups, 8, tiles, LANES).transpose(0, 1, 3, 2, 4)
    sem, real = pltpu.SemaphoreType.DMA, jnp.float32
    piece = (groups, 2, per_piece, 8, LANES)
    return pl.pallas_call(
        functools.partial(render, planes * nd),
        out_shape=jax.ShapeDtypeStruct((4, rows, width // nd), real),
        in_specs=[pl.BlockSpec(memory_space=pltpu.SMEM)] + [pl.BlockSpec(memory_space=pl.ANY)] * 2,
        out_specs=pl.BlockSpec(memory_space=pltpu.VMEM),
        scratch_shapes=[
            pltpu.SMEM((3,), real),
            pltpu.VMEM((planes, tiles + 2, rows + 2 * TOP, LANES), real),
            pltpu.VMEM((2, groups, tiles, 8, LANES), real),
            pltpu.VMEM((tiles, 3, rows // 2, LANES), real),
            pltpu.VMEM((nd, *piece), real),
            pltpu.VMEM((chips, *piece), real),
            pltpu.VMEM((chips, *piece), real),
            pltpu.VMEM((chips, *piece), real),
            sem,
            sem((nd,)),
            *[sem] * 2,
            sem((nd,)),
            *[sem, sem((nd,))] * 2,
            *[pltpu.SemaphoreType.REGULAR] * 2,
            sem,
            sem((chips, 3)),
            *[sem] * 3,
        ],
        compiler_params=pltpu.CompilerParams(
            collective_id=0, has_side_effects=True, vmem_limit_bytes=52 * 2**20
        ),
    )(absorption, *(pltpu.with_memory_space_constraint(x, pltpu.HBM) for x in (emission, tiled)))


def solution(mesh):
    placed = (P("depth", "row", None), P(), P())
    return jax.shard_map(
        per_device, mesh=mesh, in_specs=placed, out_specs=P(None, "row", "depth"), check_vma=False
    )
```

```python
import functools
import math

import jax
import jax.numpy as jnp
from jax import lax
from jax.experimental import pallas as pl
from jax.experimental.pallas import tpu as pltpu
from jax.sharding import PartitionSpec as P

MESH = pl.DeviceIdType.MESH
LANES = 128
HIGH, LOW, INNER = range(3)
LINE = 8
TOP = 8


def chain(i, values):
    out = values[-1]
    for at in range(len(values) - 2, -1, -1):
        out = jnp.where(i == at, values[at], out)
    return out


def lagging(count, lag):
    ahead = [(2 * k, 0, k) for k in range(count)]
    behind = [(2 * (k + lag) - 1, 1, k) for k in range(count)]
    return [turn for _, *turn in sorted(ahead + behind)]


def each(count, body):
    def run(i, carry):
        body(i)
        return carry

    lax.fori_loop(0, count, run, 0)


def render(
    depth_total, absorption, emission_in, density, out, emission, vol, planes_in, mid, stage, merged,
    sibling, chips_in, emission_sem, local_sem, up_send, down_send, planes_recv, low_send, low_recv,
    high_send, high_recv, late_sem, twin_sem, sib_send, sib_recv, sib_own_recv, out_send, out_recv,
):
    planes, groups, tiles = density.shape[:3]
    rows = 8 * groups
    body_rows = pl.ds(TOP, rows)
    last = planes - 1
    nd, nr = lax.axis_size("depth"), lax.axis_size("row")
    d, r = lax.axis_index("depth"), lax.axis_index("row")
    chips = nd // 2
    chip, core = d // 2, d % 2
    twin = d + 1 - 2 * core
    per_piece = tiles // nd
    inner_groups = range(1, groups - 1)
    first_of_line = (r % LINE == 0) & (r > 0)
    last_of_line = (r % LINE == LINE - 1) & (r < nr - 1)
    before_last = (r % LINE == LINE - 2) & (r < nr - 2)
    greets, hears = last_of_line & (core == 0), last_of_line & (core == 1)
    PARTS = pl.ds(groups - 1, 1), pl.ds(0, 1), pl.ds(1, groups - 2)

    def tiles_of(piece):
        return pl.ds(piece * per_piece, per_piece)

    def local_copy(piece, g):
        return pltpu.make_async_copy(
            density.at[:, g, tiles_of(piece)],
            vol.at[:, pl.ds(piece * per_piece + 1, per_piece), pl.ds(TOP + 8 * g, 8), :],
            local_sem.at[piece],
        )

    def wait_local(piece):
        block = vol.at[:, pl.ds(piece * per_piece + 1, per_piece), body_rows, :]
        pltpu.make_async_copy(block, block, local_sem.at[piece]).wait()

    near, far = planes_in.at[0], planes_in.at[1]

    def z_copy(piece, up):
        return pltpu.make_async_remote_copy(
            src_ref=density.at[last if up else 0, :, tiles_of(piece)],
            dst_ref=(near if up else far).at[:, tiles_of(piece)],
            send_sem=up_send if up else down_send, recv_sem=planes_recv.at[piece],
            device_id={"depth": d + 1 if up else d - 1}, device_id_type=MESH,
        )

    def wait_planes(piece):
        def arrived(ref):
            pltpu.make_async_copy(ref, ref, planes_recv.at[piece]).wait()

        pl.when(d == 0)(lambda: arrived(far.at[:, tiles_of(piece)]))
        pl.when(d == nd - 1)(lambda: arrived(near.at[:, tiles_of(piece)]))
        pl.when((d > 0) & (d < nd - 1))(lambda: arrived(planes_in.at[:, :, tiles_of(piece)]))

    def y_copy(piece, up):
        g, y, target = (groups - 1, 7, TOP - 1) if up else (0, 0, TOP + rows)
        send, got = (low_send, low_recv) if up else (high_send, high_recv)
        return pltpu.make_async_remote_copy(
            src_ref=density.at[:, g, tiles_of(piece), y, :],
            dst_ref=vol.at[:, pl.ds(piece * per_piece + 1, per_piece), target, :],
            send_sem=send, recv_sem=got.at[piece],
            device_id={"row": r + 1 if up else r - 1}, device_id_type=MESH,
        )

    def sibling_copy(target_chip, part):
        return pltpu.make_async_remote_copy(
            src_ref=stage.at[target_chip * 2 + 1 - core, PARTS[part]],
            dst_ref=sibling.at[target_chip, PARTS[part]], send_sem=sib_send,
            recv_sem=sib_recv.at[target_chip, part], device_id={"depth": twin}, device_id_type=MESH,
        )

    def sibling_own_copy(part):
        return pltpu.make_async_remote_copy(
            src_ref=stage.at[twin, PARTS[part]], dst_ref=sibling.at[chip, PARTS[part]],
            send_sem=sib_send, recv_sem=sib_own_recv, device_id={"depth": twin}, device_id_type=MESH,
        )

    def chip_copy(other, part):
        return pltpu.make_async_remote_copy(
            src_ref=merged.at[other, PARTS[part]], dst_ref=chips_in.at[chip, PARTS[part]],
            send_sem=out_send, recv_sem=out_recv, device_id={"depth": other * 2 + core}, device_id_type=MESH,
        )

    def arrived(ref, sem):
        pltpu.make_async_copy(ref, ref, sem).wait()

    def order(step, device=d):
        mine = ((step >= chips - 1) & (step < nd - 2)) | (step == nd - 1)
        at, core = device // 2, device % 2
        other = step % (chips - 1)
        other = other + jnp.where(other >= at, 1, 0)
        return jnp.where(step < nd - 2, other, at), jnp.where(mine, core, 1 - core)

    def piece_at(step, device=d):
        owner_chip, owner_core = order(step, device)
        return owner_chip * 2 + owner_core

    barrier = pltpu.get_barrier_semaphore()

    def signal(depth, row):
        pl.semaphore_signal(barrier, inc=1, device_id={"depth": depth, "row": row}, device_id_type=MESH)

    signal(twin, r)
    for apart in range(1, chips):
        signal((chip + apart) % chips * 2 + jnp.where(last_of_line, 1, core), r)
    pl.when(jnp.logical_not(last_of_line))(lambda: signal((d + nd - 1 + 2 * core) % nd, r))
    pl.when(r > 0)(lambda: signal(jnp.where(first_of_line, chip * 2, d), r - 1))
    pl.when((r < nr - 1) & jnp.logical_not(last_of_line))(
        lambda: signal(jnp.where(before_last, chip * 2 + 1, d), r + 1)
    )
    below = jnp.where((r > 0) & jnp.logical_not(first_of_line), 1, 0)
    above = jnp.where(r < nr - 1, 1, 0)

    def start_local(piece):
        for g in range(groups):
            local_copy(piece, g).start()

    ahead = jnp.where(last_of_line, 2, nd)
    each(ahead, start_local)
    emission_copy = pltpu.make_async_copy(emission_in, emission, emission_sem)
    emission_copy.start()

    blank = jnp.zeros((planes, rows, LANES), jnp.float32)
    vol[:, 0, pl.ds(TOP, rows), :] = blank
    vol[:, tiles + 1, pl.ds(TOP, rows), :] = blank

    def clear_plane(ref):
        ref[...] = jnp.zeros(ref.shape, jnp.float32)

    def clear_row(y):
        def one(z):
            vol[z, :, y, :] = jnp.zeros((tiles + 2, LANES), jnp.float32)

        each(planes, one)

    pl.when(d == 0)(lambda: clear_plane(near))
    pl.when(d == nd - 1)(lambda: clear_plane(far))
    pl.when(r == 0)(lambda: clear_row(TOP - 1))
    pl.when(r == nr - 1)(lambda: clear_row(TOP + rows))

    def start_halos(step):
        piece = piece_at(step)
        pl.when(d < nd - 1)(lambda: z_copy(piece_at(step, d + 1), True).start())
        pl.when(d > 0)(lambda: z_copy(piece_at(step, d - 1), False).start())
        pl.when((r < nr - 1) & jnp.logical_not(last_of_line))(lambda: y_copy(piece, True).start())
        pl.when((r > 0) & jnp.logical_not(first_of_line))(lambda: y_copy(piece, False).start())

    def start_late(step):
        y_copy(piece_at(step), False).start()

    def open_late():
        pl.semaphore_wait(late_sem, 1)
        each(nd, start_late)

    def tell_twin():
        pl.semaphore_signal(twin_sem, inc=1, device_id={"depth": twin}, device_id_type=MESH)

    @pl.when(jnp.logical_not(hears))
    def _():
        pl.semaphore_wait(barrier, jnp.where(greets, 3, 5 + below + above))

    pl.when(greets)(tell_twin)
    pl.when(hears)(lambda: pl.semaphore_wait(twin_sem, 1))

    @pl.when(last_of_line)
    def _():
        pl.semaphore_signal(late_sem, inc=1, device_id={"row": r + 1}, device_id_type=MESH)
        each(nd, lambda step: y_copy(piece_at(step), True).start())
        each(nd - 2, lambda piece: start_local(piece + 2))

    @pl.when(hears)
    def _():
        pl.semaphore_wait(barrier, 2 * chips + 1)
        tell_twin()

    pl.when(greets)(lambda: pl.semaphore_wait(twin_sem, 1))
    each(nd, start_halos)

    rate = absorption[0] * (-math.log2(math.e) / depth_total)
    lane = lax.broadcasted_iota(jnp.int32, (8, LANES), 1)
    is_first, is_last = lane == 0, lane == LANES - 1
    zero, one = jnp.zeros((8, LANES), jnp.float32), jnp.ones((8, LANES), jnp.float32)

    def load(tile, z, g, shift=0):
        return vol[z, tile + 1, pl.ds(TOP + 8 * g + shift, 8), :]

    def shading(unit, z, before, c, after):
        tile, g = unit
        left = pltpu.roll(jnp.where(is_last, load(tile - 1, z, g), c), 1, 1)
        right = pltpu.roll(jnp.where(is_first, load(tile + 1, z, g), c), LANES - 1, 1)
        dx = right - left
        dy = load(tile, z, g, 1) - load(tile, z, g, -1)
        dz = after - before
        along = jnp.abs(dz + 0.9375 * dy + 0.75 * dx)
        return along * lax.rsqrt(dz * dz + dy * dy + dx * dx + 4.0)

    def advance(units, z, carry, after):
        before, cur, total, through, shine = ([*part] for part in carry)
        for i, unit in enumerate(units):
            shade = shading(unit, z, before[i], cur[i], after[i])
            total[i] = total[i] + cur[i]
            beyond = jnp.exp2(total[i] * rate)
            shine[i] = shine[i] + (through[i] - beyond) * shade
            through[i] = beyond
        return tuple(tuple(part) for part in (cur, after, total, through, shine))

    def middle(units, carry):
        def step(z, carry):
            return advance(units, z, carry, [load(t, z + 1, g) for t, g in units])

        return lax.fori_loop(1, last, step, carry, unroll=True)

    def lit_of(through, shine):
        return 0.25 * (1.0 - through) + 0.48 * shine

    wait_local(0)

    def inner(piece):
        pl.when(piece < nd - 1)(lambda: wait_local(piece + 1))
        units = [(piece * per_piece + part, g) for part in range(per_piece) for g in inner_groups]
        first = tuple(load(t, 0, g) for t, g in units)
        carry = (
            first, tuple(load(t, 1, g) for t, g in units), first,
            tuple(jnp.exp2(f * rate) for f in first), (zero,) * len(units),
        )
        _, cur, total, through, shine = middle(units, carry)
        for i, (t, g) in enumerate(units):
            at = pl.ds(8 * (g - 1), 8)
            beyond = jnp.exp2((total[i] + cur[i]) * rate)
            mid[t, 0, at, :] = shine[i]
            mid[t, 1, at, :] = beyond
            mid[t, 2, at, :] = through[i] - beyond

    each(nd, inner)

    def store(piece, side, g, lit, through):
        stage[piece, g, 0, side] = lit
        stage[piece, g, 1, side] = through

    def ends(piece):
        for part in range(per_piece):
            for g in inner_groups:
                tile = piece * per_piece + part
                unit, at = (tile, g), pl.ds(8 * (g - 1), 8)
                first = load(tile, 0, g)
                shine = mid[tile, 0, at, :]
                shine += (1.0 - jnp.exp2(first * rate)) * shading(unit, 0, planes_in[0, g, tile], first, load(tile, 1, g))
                shine += mid[tile, 2, at, :] * shading(
                    unit, last, load(tile, last - 1, g), load(tile, last, g), planes_in[1, g, tile]
                )
                through = mid[tile, 1, at, :]
                store(piece, part, g, lit_of(through, shine), through)

    def outer(piece, g):
        units = [(piece * per_piece + part, g) for part in range(per_piece)]
        carry = (
            tuple(planes_in[0, g, t] for t, g in units), tuple(load(t, 0, g) for t, g in units),
            (zero,) * len(units), (one,) * len(units), (zero,) * len(units),
        )
        carry = advance(units, 0, carry, [load(t, 1, g) for t, g in units])
        carry = middle(units, carry)
        _, _, _, through, shine = advance(units, last, carry, [planes_in[1, g, t] for t, g in units])
        for side in range(per_piece):
            store(piece, side, g, lit_of(through[side], shine[side]), through[side])

    def merge(target_chip, part):
        mine, other = stage.at[target_chip * 2 + core, PARTS[part]], sibling.at[target_chip, PARTS[part]]
        lit, through = mine[:, 0], mine[:, 1]
        lit_other, through_other = other[:, 0], other[:, 1]
        front = core == 0
        lit_all = jnp.where(front, lit, lit_other) + jnp.where(front, through, through_other) * jnp.where(
            front, lit_other, lit
        )
        return lit_all, through * through_other

    def dispatch(step, part):
        target, owner = order(step)

        @pl.when((owner != core) & (target != chip))
        def _():
            sibling_copy(target, part).start()

        @pl.when((owner != core) & (target == chip))
        def _():
            sibling_own_copy(part).start()

        @pl.when((owner == core) & (target != chip))
        def _():
            sibling_copy(target, part).wait_recv()
            merged[target, PARTS[part], 0], merged[target, PARTS[part], 1] = merge(target, part)
            chip_copy(target, part).start()

    wait_planes(piece_at(0))
    ends(piece_at(0))
    dispatch(0, INNER)

    def high_step(step):
        piece, later = piece_at(step), piece_at(jnp.minimum(step + 1, nd - 1))
        pl.when(r < nr - 1)(lambda: y_copy(piece, False).wait_recv())
        ends(later)
        outer(piece, groups - 1)
        dispatch(step, HIGH)
        pl.when(step < nd - 1)(lambda: dispatch(step + 1, INNER))

    def low_step(step):
        piece = piece_at(step)
        pl.when(r > 0)(lambda: y_copy(piece, True).wait_recv())
        outer(piece, 0)
        dispatch(step, LOW)

    def outer_step(i):
        pl.when(first_of_line & (i == 2))(open_late)
        trails, step = i % 2, i // 2
        for rows_of, lag in ((first_of_line, 4), (last_of_line, 3)):
            turns = lagging(nd - 2, lag) + [[side, k] for k in (nd - 2, nd - 1) for side in (0, 1)]
            trails = jnp.where(rows_of, chain(i, [t for t, _ in turns]), trails)
            step = jnp.where(rows_of, chain(i, [k for _, k in turns]), step)
        low = jnp.where(last_of_line, 1 - trails, trails)
        pl.when((trails == 0) & (step < nd - 1))(lambda: wait_planes(piece_at(step + 1)))
        pl.when(low == 0)(lambda: high_step(step))
        pl.when(low == 1)(lambda: low_step(step))

    each(2 * nd, outer_step)

    def sent(ref, sem):
        pltpu.make_async_remote_copy(
            src_ref=ref, dst_ref=ref, send_sem=sem, recv_sem=out_recv,
            device_id={"depth": twin}, device_id_type=MESH,
        ).wait_send()

    pl.when(d < nd - 1)(lambda: sent(near, up_send))
    pl.when(d > 0)(lambda: sent(far, down_send))
    halo_row = vol.at[:, pl.ds(1, tiles), TOP, :]
    pl.when(r < nr - 1)(lambda: sent(halo_row, low_send))
    pl.when(r > 0)(lambda: sent(halo_row, high_send))
    sent(sibling, sib_send)
    emission_copy.wait()
    arrived(sibling.at[chip], sib_own_recv)
    for part in (HIGH, LOW, INNER):
        chips_in[chip, PARTS[part], 0], chips_in[chip, PARTS[part], 1] = merge(chip, part)
    others = merged.at[pl.ds(0, chips - 1)]
    sent(others, out_send)
    arrived(others, out_recv)

    for g in range(groups):
        for side in range(per_piece):
            lit, through = chips_in[0, g, 0, side], chips_in[0, g, 1, side]
            for s in range(1, chips):
                lit = lit + through * chips_in[s, g, 0, side]
                through = through * chips_in[s, g, 1, side]
            place = pl.ds(8 * g, 8), pl.ds(side * LANES, LANES)
            for c in range(3):
                out[(c, *place)] = emission[c] * lit
            out[(3, *place)] = 1.0 - through


def per_device(density, emission, absorption):
    nd = lax.axis_size("depth")
    chips = nd // 2
    planes, rows, width = density.shape
    tiles, groups = width // LANES, rows // 8
    per_piece = tiles // nd
    tiled = density.reshape(planes, groups, 8, tiles, LANES).transpose(0, 1, 3, 2, 4)
    sem, real = pltpu.SemaphoreType.DMA, jnp.float32
    piece = (groups, 2, per_piece, 8, LANES)
    return pl.pallas_call(
        functools.partial(render, planes * nd),
        out_shape=jax.ShapeDtypeStruct((4, rows, width // nd), real),
        in_specs=[pl.BlockSpec(memory_space=pltpu.SMEM)] + [pl.BlockSpec(memory_space=pl.ANY)] * 2,
        out_specs=pl.BlockSpec(memory_space=pltpu.VMEM),
        scratch_shapes=[
            pltpu.SMEM((3,), real),
            pltpu.VMEM((planes, tiles + 2, rows + 2 * TOP, LANES), real),
            pltpu.VMEM((2, groups, tiles, 8, LANES), real),
            pltpu.VMEM((tiles, 3, rows // 2, LANES), real),
            pltpu.VMEM((nd, *piece), real),
            pltpu.VMEM((chips, *piece), real),
            pltpu.VMEM((chips, *piece), real),
            pltpu.VMEM((chips, *piece), real),
            sem,
            sem((nd,)),
            *[sem] * 2,
            sem((nd,)),
            *[sem, sem((nd,))] * 2,
            *[pltpu.SemaphoreType.REGULAR] * 2,
            sem,
            sem((chips, 3)),
            *[sem] * 3,
        ],
        compiler_params=pltpu.CompilerParams(
            collective_id=0, has_side_effects=True, vmem_limit_bytes=52 * 2**20
        ),
    )(absorption, *(pltpu.with_memory_space_constraint(x, pltpu.HBM) for x in (emission, tiled)))


def solution(mesh):
    placed = (P("depth", "row", None), P(), P())
    return jax.shard_map(
        per_device, mesh=mesh, in_specs=placed, out_specs=P(None, "row", "depth"), check_vma=False
    )
```

```python
import functools
import math

import jax
import jax.numpy as jnp
from jax import lax
from jax.experimental import pallas as pl
from jax.experimental.pallas import tpu as pltpu
from jax.sharding import PartitionSpec as P

MESH = pl.DeviceIdType.MESH
LANES = 128
HIGH, LOW, INNER = range(3)
LINE = 8
TOP = 8


def chain(i, values):
    out = values[-1]
    for at in range(len(values) - 2, -1, -1):
        out = jnp.where(i == at, values[at], out)
    return out


def lagging(count, lag):
    ahead = [(2 * k, 0, k) for k in range(count)]
    behind = [(2 * (k + lag) - 1, 1, k) for k in range(count)]
    return [turn for _, *turn in sorted(ahead + behind)]


def each(count, body):
    def run(i, carry):
        body(i)
        return carry

    lax.fori_loop(0, count, run, 0)


def render(
    depth_total, absorption, emission_in, density, out, emission, vol, planes_in, mid, stage, merged,
    sibling, chips_in, emission_sem, local_sem, up_send, down_send, planes_recv, low_send, low_recv,
    high_send, high_recv, late_sem, twin_sem, sib_send, sib_recv, sib_own_recv, out_send, out_recv,
):
    planes, groups, tiles = density.shape[:3]
    rows = 8 * groups
    body_rows = pl.ds(TOP, rows)
    last = planes - 1
    nd, nr = lax.axis_size("depth"), lax.axis_size("row")
    d, r = lax.axis_index("depth"), lax.axis_index("row")
    chips = nd // 2
    chip, core = d // 2, d % 2
    twin = d + 1 - 2 * core
    per_piece = tiles // nd
    inner_groups = range(1, groups - 1)
    first_of_line = (r % LINE == 0) & (r > 0)
    last_of_line = (r % LINE == LINE - 1) & (r < nr - 1)
    before_last = (r % LINE == LINE - 2) & (r < nr - 2)
    greets, hears = last_of_line & (core == 0), last_of_line & (core == 1)
    PARTS = pl.ds(groups - 1, 1), pl.ds(0, 1), pl.ds(1, groups - 2)

    def tiles_of(piece):
        return pl.ds(piece * per_piece, per_piece)

    def local_copy(piece, g):
        return pltpu.make_async_copy(
            density.at[:, g, tiles_of(piece)],
            vol.at[:, pl.ds(piece * per_piece + 1, per_piece), pl.ds(TOP + 8 * g, 8), :],
            local_sem.at[piece],
        )

    def wait_local(piece):
        block = vol.at[:, pl.ds(piece * per_piece + 1, per_piece), body_rows, :]
        pltpu.make_async_copy(block, block, local_sem.at[piece]).wait()

    near, far = planes_in.at[0], planes_in.at[1]

    def z_copy(piece, up):
        return pltpu.make_async_remote_copy(
            src_ref=density.at[last if up else 0, :, tiles_of(piece)],
            dst_ref=(near if up else far).at[:, tiles_of(piece)],
            send_sem=up_send if up else down_send, recv_sem=planes_recv.at[piece],
            device_id={"depth": d + 1 if up else d - 1}, device_id_type=MESH,
        )

    def wait_planes(piece):
        def arrived(ref):
            pltpu.make_async_copy(ref, ref, planes_recv.at[piece]).wait()

        pl.when(d == 0)(lambda: arrived(far.at[:, tiles_of(piece)]))
        pl.when(d == nd - 1)(lambda: arrived(near.at[:, tiles_of(piece)]))
        pl.when((d > 0) & (d < nd - 1))(lambda: arrived(planes_in.at[:, :, tiles_of(piece)]))

    def y_copy(piece, up):
        g, y, target = (groups - 1, 7, TOP - 1) if up else (0, 0, TOP + rows)
        send, got = (low_send, low_recv) if up else (high_send, high_recv)
        return pltpu.make_async_remote_copy(
            src_ref=density.at[:, g, tiles_of(piece), y, :],
            dst_ref=vol.at[:, pl.ds(piece * per_piece + 1, per_piece), target, :],
            send_sem=send, recv_sem=got.at[piece],
            device_id={"row": r + 1 if up else r - 1}, device_id_type=MESH,
        )

    def sibling_copy(target_chip, part):
        return pltpu.make_async_remote_copy(
            src_ref=stage.at[target_chip * 2 + 1 - core, PARTS[part]],
            dst_ref=sibling.at[target_chip, PARTS[part]], send_sem=sib_send,
            recv_sem=sib_recv.at[target_chip, part], device_id={"depth": twin}, device_id_type=MESH,
        )

    def sibling_own_copy(part):
        return pltpu.make_async_remote_copy(
            src_ref=stage.at[twin, PARTS[part]], dst_ref=sibling.at[chip, PARTS[part]],
            send_sem=sib_send, recv_sem=sib_own_recv, device_id={"depth": twin}, device_id_type=MESH,
        )

    def chip_copy(other, part):
        return pltpu.make_async_remote_copy(
            src_ref=merged.at[other, PARTS[part]], dst_ref=chips_in.at[chip, PARTS[part]],
            send_sem=out_send, recv_sem=out_recv, device_id={"depth": other * 2 + core}, device_id_type=MESH,
        )

    def arrived(ref, sem):
        pltpu.make_async_copy(ref, ref, sem).wait()

    def order(step, device=d):
        mine = ((step >= chips - 1) & (step < nd - 2)) | (step == nd - 1)
        at, core = device // 2, device % 2
        other = step % (chips - 1)
        other = other + jnp.where(other >= at, 1, 0)
        return jnp.where(step < nd - 2, other, at), jnp.where(mine, core, 1 - core)

    def piece_at(step, device=d):
        owner_chip, owner_core = order(step, device)
        return owner_chip * 2 + owner_core

    barrier = pltpu.get_barrier_semaphore()

    def signal(depth, row):
        pl.semaphore_signal(barrier, inc=1, device_id={"depth": depth, "row": row}, device_id_type=MESH)

    signal(twin, r)
    for apart in range(1, chips):
        signal((chip + apart) % chips * 2 + jnp.where(last_of_line, 1, core), r)
    pl.when(jnp.logical_not(last_of_line))(lambda: signal((d + nd - 1 + 2 * core) % nd, r))
    pl.when(r > 0)(lambda: signal(jnp.where(first_of_line, chip * 2, d), r - 1))
    pl.when((r < nr - 1) & jnp.logical_not(last_of_line))(
        lambda: signal(jnp.where(before_last, chip * 2 + 1, d), r + 1)
    )
    below = jnp.where((r > 0) & jnp.logical_not(first_of_line), 1, 0)
    above = jnp.where(r < nr - 1, 1, 0)

    def start_local(piece):
        for g in range(groups):
            local_copy(piece, g).start()

    ahead = jnp.where(last_of_line, 2, nd)
    each(ahead, start_local)
    emission_copy = pltpu.make_async_copy(emission_in, emission, emission_sem)
    emission_copy.start()

    def start_halos(step):
        piece = piece_at(step)
        pl.when(d < nd - 1)(lambda: z_copy(piece_at(step, d + 1), True).start())
        pl.when(d > 0)(lambda: z_copy(piece_at(step, d - 1), False).start())
        pl.when((r < nr - 1) & jnp.logical_not(last_of_line))(lambda: y_copy(piece, True).start())
        pl.when((r > 0) & jnp.logical_not(first_of_line))(lambda: y_copy(piece, False).start())

    def start_late(step):
        y_copy(piece_at(step), False).start()

    def open_late():
        pl.semaphore_wait(late_sem, 1)
        each(nd, start_late)

    def tell_twin():
        pl.semaphore_signal(twin_sem, inc=1, device_id={"depth": twin}, device_id_type=MESH)

    @pl.when(jnp.logical_not(hears))
    def _():
        pl.semaphore_wait(barrier, jnp.where(greets, 3, 5 + below + above))

    pl.when(greets)(tell_twin)
    pl.when(hears)(lambda: pl.semaphore_wait(twin_sem, 1))

    @pl.when(last_of_line)
    def _():
        pl.semaphore_signal(late_sem, inc=1, device_id={"row": r + 1}, device_id_type=MESH)
        each(nd, lambda step: y_copy(piece_at(step), True).start())
        each(nd - 2, lambda piece: start_local(piece + 2))

    @pl.when(hears)
    def _():
        pl.semaphore_wait(barrier, 2 * chips + 1)
        tell_twin()

    pl.when(greets)(lambda: pl.semaphore_wait(twin_sem, 1))
    each(nd, start_halos)

    blank = jnp.zeros((planes, rows, LANES), jnp.float32)
    vol[:, 0, pl.ds(TOP, rows), :] = blank
    vol[:, tiles + 1, pl.ds(TOP, rows), :] = blank

    def clear_plane(ref):
        ref[...] = jnp.zeros(ref.shape, jnp.float32)

    def clear_row(y):
        def one(z):
            vol[z, :, y, :] = jnp.zeros((tiles + 2, LANES), jnp.float32)

        each(planes, one)

    pl.when(d == 0)(lambda: clear_plane(near))
    pl.when(d == nd - 1)(lambda: clear_plane(far))
    pl.when(r == 0)(lambda: clear_row(TOP - 1))
    pl.when(r == nr - 1)(lambda: clear_row(TOP + rows))

    rate = absorption[0] * (-math.log2(math.e) / depth_total)
    lane = lax.broadcasted_iota(jnp.int32, (8, LANES), 1)
    is_first, is_last = lane == 0, lane == LANES - 1
    zero, one = jnp.zeros((8, LANES), jnp.float32), jnp.ones((8, LANES), jnp.float32)

    def load(tile, z, g, shift=0):
        return vol[z, tile + 1, pl.ds(TOP + 8 * g + shift, 8), :]

    def shading(unit, z, before, c, after):
        tile, g = unit
        left = pltpu.roll(jnp.where(is_last, load(tile - 1, z, g), c), 1, 1)
        right = pltpu.roll(jnp.where(is_first, load(tile + 1, z, g), c), LANES - 1, 1)
        dx = right - left
        dy = load(tile, z, g, 1) - load(tile, z, g, -1)
        dz = after - before
        along = jnp.abs(dz + 0.9375 * dy + 0.75 * dx)
        return along * lax.rsqrt(dz * dz + dy * dy + dx * dx + 4.0)

    def advance(units, z, carry, after):
        before, cur, total, through, shine = ([*part] for part in carry)
        for i, unit in enumerate(units):
            shade = shading(unit, z, before[i], cur[i], after[i])
            total[i] = total[i] + cur[i]
            beyond = jnp.exp2(total[i] * rate)
            shine[i] = shine[i] + (through[i] - beyond) * shade
            through[i] = beyond
        return tuple(tuple(part) for part in (cur, after, total, through, shine))

    def middle(units, carry):
        def step(z, carry):
            return advance(units, z, carry, [load(t, z + 1, g) for t, g in units])

        return lax.fori_loop(1, last, step, carry, unroll=True)

    def lit_of(through, shine):
        return 0.25 * (1.0 - through) + 0.48 * shine

    wait_local(0)

    def inner(piece):
        pl.when(piece < nd - 1)(lambda: wait_local(piece + 1))
        units = [(piece * per_piece + part, g) for part in range(per_piece) for g in inner_groups]
        first = tuple(load(t, 0, g) for t, g in units)
        carry = (
            first, tuple(load(t, 1, g) for t, g in units), first,
            tuple(jnp.exp2(f * rate) for f in first), (zero,) * len(units),
        )
        _, cur, total, through, shine = middle(units, carry)
        for i, (t, g) in enumerate(units):
            at = pl.ds(8 * (g - 1), 8)
            beyond = jnp.exp2((total[i] + cur[i]) * rate)
            mid[t, 0, at, :] = shine[i]
            mid[t, 1, at, :] = beyond
            mid[t, 2, at, :] = through[i] - beyond

    each(nd, inner)

    def store(piece, side, g, lit, through):
        stage[piece, g, 0, side] = lit
        stage[piece, g, 1, side] = through

    def ends(piece):
        for part in range(per_piece):
            for g in inner_groups:
                tile = piece * per_piece + part
                unit, at = (tile, g), pl.ds(8 * (g - 1), 8)
                first = load(tile, 0, g)
                shine = mid[tile, 0, at, :]
                shine += (1.0 - jnp.exp2(first * rate)) * shading(unit, 0, planes_in[0, g, tile], first, load(tile, 1, g))
                shine += mid[tile, 2, at, :] * shading(
                    unit, last, load(tile, last - 1, g), load(tile, last, g), planes_in[1, g, tile]
                )
                through = mid[tile, 1, at, :]
                store(piece, part, g, lit_of(through, shine), through)

    def outer(piece, g):
        units = [(piece * per_piece + part, g) for part in range(per_piece)]
        carry = (
            tuple(planes_in[0, g, t] for t, g in units), tuple(load(t, 0, g) for t, g in units),
            (zero,) * len(units), (one,) * len(units), (zero,) * len(units),
        )
        carry = advance(units, 0, carry, [load(t, 1, g) for t, g in units])
        carry = middle(units, carry)
        _, _, _, through, shine = advance(units, last, carry, [planes_in[1, g, t] for t, g in units])
        for side in range(per_piece):
            store(piece, side, g, lit_of(through[side], shine[side]), through[side])

    def merge(target_chip, part):
        mine, other = stage.at[target_chip * 2 + core, PARTS[part]], sibling.at[target_chip, PARTS[part]]
        lit, through = mine[:, 0], mine[:, 1]
        lit_other, through_other = other[:, 0], other[:, 1]
        front = core == 0
        lit_all = jnp.where(front, lit, lit_other) + jnp.where(front, through, through_other) * jnp.where(
            front, lit_other, lit
        )
        return lit_all, through * through_other

    def dispatch(step, part):
        target, owner = order(step)

        @pl.when((owner != core) & (target != chip))
        def _():
            sibling_copy(target, part).start()

        @pl.when((owner != core) & (target == chip))
        def _():
            sibling_own_copy(part).start()

        @pl.when((owner == core) & (target != chip))
        def _():
            sibling_copy(target, part).wait_recv()
            merged[target, PARTS[part], 0], merged[target, PARTS[part], 1] = merge(target, part)
            chip_copy(target, part).start()

    wait_planes(piece_at(0))
    ends(piece_at(0))
    dispatch(0, INNER)

    def high_step(step):
        piece, later = piece_at(step), piece_at(jnp.minimum(step + 1, nd - 1))
        pl.when(r < nr - 1)(lambda: y_copy(piece, False).wait_recv())
        ends(later)
        outer(piece, groups - 1)
        dispatch(step, HIGH)
        pl.when(step < nd - 1)(lambda: dispatch(step + 1, INNER))

    def low_step(step):
        piece = piece_at(step)
        pl.when(r > 0)(lambda: y_copy(piece, True).wait_recv())
        outer(piece, 0)
        dispatch(step, LOW)

    def outer_step(i):
        pl.when(first_of_line & (i == 2))(open_late)
        trails, step = i % 2, i // 2
        for rows_of, lag in ((first_of_line, 4), (last_of_line, 3)):
            turns = lagging(nd - 2, lag) + [[side, k] for k in (nd - 2, nd - 1) for side in (0, 1)]
            trails = jnp.where(rows_of, chain(i, [t for t, _ in turns]), trails)
            step = jnp.where(rows_of, chain(i, [k for _, k in turns]), step)
        low = jnp.where(last_of_line, 1 - trails, trails)
        pl.when((trails == 0) & (step < nd - 1))(lambda: wait_planes(piece_at(step + 1)))
        pl.when(low == 0)(lambda: high_step(step))
        pl.when(low == 1)(lambda: low_step(step))

    each(2 * nd, outer_step)

    def sent(ref, sem):
        pltpu.make_async_remote_copy(
            src_ref=ref, dst_ref=ref, send_sem=sem, recv_sem=out_recv,
            device_id={"depth": twin}, device_id_type=MESH,
        ).wait_send()

    pl.when(d < nd - 1)(lambda: sent(near, up_send))
    pl.when(d > 0)(lambda: sent(far, down_send))
    halo_row = vol.at[:, pl.ds(1, tiles), TOP, :]
    pl.when(r < nr - 1)(lambda: sent(halo_row, low_send))
    pl.when(r > 0)(lambda: sent(halo_row, high_send))
    sent(sibling, sib_send)
    emission_copy.wait()
    arrived(sibling.at[chip], sib_own_recv)
    for part in (HIGH, LOW, INNER):
        chips_in[chip, PARTS[part], 0], chips_in[chip, PARTS[part], 1] = merge(chip, part)
    others = merged.at[pl.ds(0, chips - 1)]
    sent(others, out_send)
    arrived(others, out_recv)

    for g in range(groups):
        for side in range(per_piece):
            lit, through = chips_in[0, g, 0, side], chips_in[0, g, 1, side]
            for s in range(1, chips):
                lit = lit + through * chips_in[s, g, 0, side]
                through = through * chips_in[s, g, 1, side]
            place = pl.ds(8 * g, 8), pl.ds(side * LANES, LANES)
            for c in range(3):
                out[(c, *place)] = emission[c] * lit
            out[(3, *place)] = 1.0 - through


def per_device(density, emission, absorption):
    nd = lax.axis_size("depth")
    chips = nd // 2
    planes, rows, width = density.shape
    tiles, groups = width // LANES, rows // 8
    per_piece = tiles // nd
    tiled = density.reshape(planes, groups, 8, tiles, LANES).transpose(0, 1, 3, 2, 4)
    sem, real = pltpu.SemaphoreType.DMA, jnp.float32
    piece = (groups, 2, per_piece, 8, LANES)
    return pl.pallas_call(
        functools.partial(render, planes * nd),
        out_shape=jax.ShapeDtypeStruct((4, rows, width // nd), real),
        in_specs=[pl.BlockSpec(memory_space=pltpu.SMEM)] + [pl.BlockSpec(memory_space=pl.ANY)] * 2,
        out_specs=pl.BlockSpec(memory_space=pltpu.VMEM),
        scratch_shapes=[
            pltpu.SMEM((3,), real),
            pltpu.VMEM((planes, tiles + 2, rows + 2 * TOP, LANES), real),
            pltpu.VMEM((2, groups, tiles, 8, LANES), real),
            pltpu.VMEM((tiles, 3, rows // 2, LANES), real),
            pltpu.VMEM((nd, *piece), real),
            pltpu.VMEM((chips, *piece), real),
            pltpu.VMEM((chips, *piece), real),
            pltpu.VMEM((chips, *piece), real),
            sem,
            sem((nd,)),
            *[sem] * 2,
            sem((nd,)),
            *[sem, sem((nd,))] * 2,
            *[pltpu.SemaphoreType.REGULAR] * 2,
            sem,
            sem((chips, 3)),
            *[sem] * 3,
        ],
        compiler_params=pltpu.CompilerParams(
            collective_id=0, has_side_effects=True, vmem_limit_bytes=52 * 2**20
        ),
    )(absorption, *(pltpu.with_memory_space_constraint(x, pltpu.HBM) for x in (emission, tiled)))


def solution(mesh):
    placed = (P("depth", "row", None), P(), P())
    return jax.shard_map(
        per_device, mesh=mesh, in_specs=placed, out_specs=P(None, "row", "depth"), check_vma=False
    )
```
